256 devices in a mesh: field: 2 (over core), sx: 8 (over y, x_lo), sy: 16 (over x_hi, z).
Axes of the slice: x: 4 (x_hi: 2, x_lo: 2; x = x_hi * 2 + x_lo), y: 4, z: 8, core: 2. Of those that a mesh axis runs over, the one named last changes fastest.
Arguments:
- inner_block: bfloat16 [4, 80, 32, 128, 128], P('field', 'sx', 'sy'), may hold values from 0.0004 to 0.03, as said below
- east_block: bfloat16 [4, 80, 32, 128, 128], P('field', 'sx', 'sy'), may hold values from 0.0004 to 0.03, as said below
- north_block: bfloat16 [4, 80, 32, 128, 128], P('field', 'sx', 'sy'), may hold values from 0.0004 to 0.03, as said below
- shift_diag: float32 [4, 80, 32, 128], P('field', 'sx', 'sy'), may hold values from 0.2 to 2
- coupling: float32 [4, 4, 80, 32, 128], P('field', None, 'sx', 'sy'), may hold values from -4 to 4
- coarse_flags: int32 [4, 80, 32, 128], P('field', 'sx', 'sy'), may hold values from 0 to 1, as said below
Outputs:
- coarse_node: bfloat16 [4, 4, 80, 32, 128, 128], P('field', None, 'sx', 'sy')
- coarse_east: bfloat16 [4, 80, 32, 128, 128], P('field', 'sx', 'sy')
- coarse_north: bfloat16 [4, 80, 32, 128, 128], P('field', 'sx', 'sy')
The draws below stay inside these ranges and needn't reach their ends.
Inputs may be any that keep to these rules, and one draw needn't show every extreme that they name: `coarse_flags`: 1 marks a coarse point of its field; the share of coarse points is drawn for each tile and field. `inner_block`: positive magnitudes. `east_block`: positive magnitudes. `north_block`: positive magnitudes.
All inputs are finite; a program needn't handle non-finite values.
Results may differ from the reference program's by a relative error of at most 0.0046.
Values may be sent and summed in bfloat16 or wider, within the bound.
A program may use at most 128 MiB of HBM per device.

```python
import math
import jax
import jax.numpy as jnp
from jax import lax

M = 128
NF = 4
NTX = 80
NTY = 32


def draw_coarse_flags(key, part):
    level_key = jax.random.fold_in(key, 11)
    node_key = jax.random.fold_in(key, 12)
    levels = jax.random.randint(level_key, (NF, NTX, NTY, 1), 0, 6)
    limit = jnp.right_shift(jnp.full(levels.shape, 64, jnp.int32), levels + 1)
    draws = jax.random.randint(node_key, (NF, NTX, NTY, M), 0, 64)
    return (draws < limit).astype(jnp.int32)


def banded_magnitudes(key, salt):
    near_key = jax.random.fold_in(key, salt)
    far_key = jax.random.fold_in(key, salt + 1)
    shape = (NF, NTX, NTY, M, M)
    width = float(max(M // 16, 2))
    nodes = jnp.arange(M, dtype=jnp.float32)
    distance = jnp.abs(nodes[:, None] - nodes[None, :])
    near = jnp.exp(jax.random.uniform(near_key, shape, jnp.float32, -0.9, 0.0))
    far = jnp.exp(jax.random.uniform(far_key, shape, jnp.float32, -1.38, 0.0))
    length = width
    value = 0.0019 * far + 0.0279 * jnp.exp(-distance / length) * near
    return value.astype(jnp.bfloat16)


def draw_inner_block(key, part):
    return banded_magnitudes(key, 21)


def draw_east_block(key, part):
    return banded_magnitudes(key, 31)


def draw_north_block(key, part):
    return banded_magnitudes(key, 41)


def shard_levels(key, extent, shards, low, top_value):
    def one(position, parts):
        heights = jax.random.uniform(jax.random.fold_in(jax.random.fold_in(key, 6), position), (parts,), jnp.float32, low / len(shards), top_value / len(shards))
        return jnp.repeat(jnp.exp(heights), extent[position] // parts).reshape((-1,) + (1,) * (len(extent) - position - 1))

    loudness = one(*shards[0])
    for cut in shards[1:]:
        loudness = loudness * one(*cut)
    return loudness


def noise(own_key, dims, spread, bound, shards=(), kind=jnp.bfloat16):
    loudness = shard_levels(own_key, dims, shards, -0.22, 0.18) if shards else 1.0
    array = jax.random.normal(own_key, dims, jnp.float32) * spread * loudness
    return jnp.minimum(jnp.maximum(array, -bound), bound).astype(kind)


def setup_inputs(seed: int = 0) -> dict:
    splits = jax.random.split(jax.random.key(seed), 7)
    return {
        "inner_block": draw_inner_block(jax.random.fold_in(splits[6], 71), 0),
        "east_block": draw_east_block(jax.random.fold_in(splits[6], 71), 0),
        "north_block": draw_north_block(jax.random.fold_in(splits[6], 71), 0),
        "shift_diag": jnp.clip(jnp.exp(math.log(2.0) - 2.3025851 * jax.random.uniform(splits[3], (NF, NTX, NTY, M), jnp.float32) ** shard_levels(splits[3], (NF, NTX, NTY, M), ((0, 2), (1, 8), (2, 16)), -0.2, 0.2)), 0.2, 2.0),
        "coupling": noise(splits[4], (NF, NF, NTX, NTY, M), 1.0, 4.0, ((0, 2), (2, 8), (3, 16)), jnp.float32),
        "coarse_flags": draw_coarse_flags(jax.random.fold_in(splits[6], 71), 0),
    }


def interpolate(matrix, shift, flags):
    tile_nodes = matrix.shape[-1]
    unit = jnp.eye(tile_nodes, dtype=bool)
    offdiag = jnp.where(unit, jnp.zeros((), matrix.dtype), matrix)
    weights = offdiag.astype(jnp.float32)
    coarse = flags.astype(jnp.float32)
    row_total = jnp.sum(weights, axis=-1)
    strong = jnp.sum(weights * coarse[..., None, :], axis=-1)
    diagonal = row_total + shift
    scaling = row_total / jnp.maximum(strong, row_total / 32.0)
    factor = (1.0 - coarse) * scaling / diagonal
    result = coarse[..., :, None] * unit.astype(jnp.float32) + factor[..., :, None] * coarse[..., None, :] * weights
    return result.astype(jnp.bfloat16), offdiag, diagonal


def product(left, right):
    return jnp.einsum('xyik,xykj->xyij', left.astype(jnp.float32), right.astype(jnp.float32), precision=lax.Precision.HIGHEST)


def transposed(left, right):
    return jnp.einsum('xyia,xyib->xyab', left.astype(jnp.float32), right.astype(jnp.float32), precision=lax.Precision.HIGHEST)


def reference(inner_block, east_block, north_block, shift_diag, coupling, coarse_flags):
    all_interp = lax.map(lambda index: interpolate(inner_block[index], shift_diag[index], coarse_flags[index])[0], jnp.arange(NF, dtype=jnp.int32))

    def field_rows(row_field):
        interp, offdiag, diagonal = interpolate(inner_block[row_field], shift_diag[row_field], coarse_flags[row_field])
        own_term = diagonal[..., None] * interp.astype(jnp.float32) - product(offdiag, interp)

        def column(col_field):
            weighted = jnp.where(col_field == row_field, own_term, jnp.zeros_like(own_term))
            weighted = weighted + coupling[row_field, col_field][..., None] * all_interp[col_field].astype(jnp.float32)
            return transposed(interp, weighted.astype(jnp.bfloat16)).astype(jnp.bfloat16)

        node_rows = lax.map(column, jnp.arange(NF, dtype=jnp.int32))
        east_interp = jnp.concatenate([interp[1:], jnp.zeros_like(interp[:1])], axis=0)
        east_image = product(east_block[row_field], east_interp).astype(jnp.bfloat16)
        east_rows = (-transposed(interp, east_image)).astype(jnp.bfloat16)
        north_interp = jnp.concatenate([interp[:, 1:], jnp.zeros_like(interp[:, :1])], axis=1)
        north_image = product(north_block[row_field], north_interp).astype(jnp.bfloat16)
        north_rows = (-transposed(interp, north_image)).astype(jnp.bfloat16)
        return node_rows, east_rows, north_rows

    coarse_node, coarse_east, coarse_north = lax.map(field_rows, jnp.arange(NF, dtype=jnp.int32))
    return (coarse_node, coarse_east, coarse_north)
```

```python
import jax
import jax.numpy as jnp
from jax import lax
from jax.experimental import pallas as pl
from jax.experimental.pallas import tpu as pltpu
from jax.sharding import PartitionSpec as P

BF = jnp.bfloat16
F32 = jnp.float32
MESH = pl.DeviceIdType.MESH
NN = (((1,), (0,)), ((), ()))
NT = (((1,), (1,)), ((), ()))
MIB = 1 << 20


def mm(left, right, dims=NN):
    return lax.dot_general(left, right, dims, preferred_element_type=F32)


def iota(shape, axis):
    return lax.broadcasted_iota(jnp.int32, shape, axis)


def one_hot(dest, nodes, fine):
    row = iota((nodes, nodes), 0).astype(F32)
    place = -1.0 - dest if fine else dest
    return jnp.where(place == row, 1.0, 0.0).astype(BF)


def exchange_kernel(
    counts, inner, east, north, shift, coupling, flags,
    q_out, other_out, node_out, east_out, north_out, zn_out, ze_out, dn_out, nef_out, nec_out,
    w_v, e_v, n_v, s_v, k_v, c_v, p_v, w0_v, a_v, d_v, de_v, zns_v, zes_v, c24_v, row_v, kt_v,
    in_sem, vec_sem, en_sem, zs_sem, zr_sem, es_sem, er_sem, ds_sem, dr_sem, ps_sem, pr_sem,
):
    nsx, nsy, fields, xs, ys, m = counts
    half = m // 2
    field, sx, sy = lax.axis_index("field"), lax.axis_index("sx"), lax.axis_index("sy")
    barrier = pltpu.get_barrier_semaphore()
    partner = {"field": 1 - field}

    loads = []
    for ref, dst, k in ((flags, c_v, 0), (shift, s_v, 1), (coupling, k_v, 2)):
        copy = pltpu.make_async_copy(ref, dst, vec_sem.at[k])
        copy.start()
        loads.append(copy)

    def inner_copy(f, x):
        return pltpu.make_async_copy(inner.at[f, x], w_v.at[f, x], in_sem.at[f, x])

    for x in range(xs):
        for f in range(fields):
            inner_copy(f, x).start()

    pl.semaphore_signal(barrier, inc=1, device_id=partner, device_id_type=MESH)

    @pl.when(sy < nsy - 1)
    def _():
        pl.semaphore_signal(barrier, inc=1, device_id={"sy": sy + 1}, device_id_type=MESH)

    @pl.when(sx < nsx - 1)
    def _():
        pl.semaphore_signal(barrier, inc=1, device_id={"sx": sx + 1}, device_id_type=MESH)

    en_loads = []
    for k, (ref, dst) in enumerate(((east, e_v), (north, n_v))):
        copy = pltpu.make_async_copy(ref, dst, en_sem.at[k])
        copy.start()
        en_loads.append(copy)

    eye = iota((m, m), 0) == iota((m, m), 1)

    loads[0].wait()
    for f in range(fields):
        for x in range(xs):
            c24_v[f * xs + x : f * xs + x + 1, :] = c_v[f, x, 0:1, :].astype(F32)
        for y in range(ys):
            r = fields * xs + f * ys + y
            c24_v[r : r + 1, :] = c_v[f, 0, y : y + 1, :].astype(F32)
    rows = fields * xs + fields * ys
    c24 = c24_v[...]
    before = jnp.where(iota((m, m), 0) < iota((m, m), 1), 1.0, 0.0).astype(BF)
    rank_c = mm(c24.astype(BF), before)
    count = jnp.sum(c24, axis=1, keepdims=True)
    short = jnp.minimum(count, m - count)
    rank = jnp.where(c24 > 0.5, rank_c, iota((rows, m), 1).astype(F32) - rank_c)
    place = jnp.where(rank < half, rank, rank + short)
    d_v[...] = jnp.where(c24 > 0.5, place, -1.0 - place)

    waits = 1 + jnp.where(sy > 0, 1, 0) + jnp.where(sx > 0, 1, 0)
    pl.semaphore_wait(barrier, waits)

    def d_copy(k):
        device = {"sy": sy - 1} if k == 0 else {"sx": sx - 1}
        return pltpu.make_async_remote_copy(
            src_ref=d_v, dst_ref=(dn_out if k == 0 else de_v), send_sem=ds_sem.at[k], recv_sem=dr_sem.at[k],
            device_id=device, device_id_type=MESH)

    def zn_copy(x):
        return pltpu.make_async_remote_copy(
            src_ref=zns_v.at[x], dst_ref=zn_out.at[x], send_sem=zs_sem.at[x], recv_sem=zr_sem.at[x],
            device_id={"sy": sy - 1}, device_id_type=MESH)

    def ze_copy():
        return pltpu.make_async_remote_copy(
            src_ref=zes_v, dst_ref=ze_out, send_sem=es_sem, recv_sem=er_sem,
            device_id={"sx": sx - 1}, device_id_type=MESH)

    def p_copy(x):
        return pltpu.make_async_remote_copy(
            src_ref=p_v.at[x], dst_ref=other_out.at[x], send_sem=ps_sem.at[x], recv_sem=pr_sem.at[x],
            device_id=partner, device_id_type=MESH)

    @pl.when(sy > 0)
    def _():
        d_copy(0).start()

    @pl.when(sx > 0)
    def _():
        d_copy(1).start()

    @pl.when(sy == nsy - 1)
    def _():
        dn_out[...] = jnp.full(dn_out.shape, -1.0, F32)
        zn_out[...] = jnp.zeros(zn_out.shape, BF)

    @pl.when(sx == nsx - 1)
    def _():
        de_v[...] = jnp.full(de_v.shape, -1.0, F32)
        ze_out[...] = jnp.zeros(ze_out.shape, BF)

    loads[1].wait()

    def squeeze(p_tiles, dests):
        folded = []
        for p, dest in zip(p_tiles, dests):
            y = mm(one_hot(dest, m, True), p).astype(BF)
            x = mm(y, one_hot(dest, m, False), NT)
            beyond = x[half:, :] + pltpu.roll(x[:half, :], half, 1)
            folded.append(x[:half, :half] + beyond.T[:half, :])
        return jnp.concatenate(folded, axis=1).astype(BF)

    def interpolate(x):
        for f in range(fields):
            inner_copy(f, x).wait()
        for f in range(fields):
            for y in range(ys):
                r = f * ys + y
                row_v[r : r + 1, :] = c_v[f, x, y : y + 1, :].astype(F32)
                row_v[4 + r : 5 + r, :] = s_v[f, x, y : y + 1, :]
        vecs = row_v[...]
        cols = vecs.T
        tiles, diags = [], []
        for f in range(fields):
            for y in range(ys):
                r = f * ys + y
                c_row = vecs[r : r + 1, :]
                w0 = jnp.where(eye, 0.0, w_v[f, x, y].astype(F32))
                total = jnp.sum(w0, axis=1, keepdims=True)
                wc = w0 * c_row
                strong = jnp.sum(wc, axis=1, keepdims=True)
                diag = total + cols[:, 4 + r : 5 + r]
                alpha = total / jnp.maximum(strong, total * (1.0 / 32.0))
                factor = (1.0 - cols[:, r : r + 1]) * alpha / diag
                p = jnp.where(eye, c_row, factor * wc)
                p_b = p.astype(BF)
                p_v[x, f, y] = p_b
                q_out[x, f, y] = p.T.astype(BF)
                w0_v[x, f, y] = w0.astype(BF)
                tiles.append(p_b)
                diags.append(diag)
        a_v[x] = jnp.concatenate(diags, axis=1)
        p_copy(x).start()
        return tiles

    def send_north(x, tiles):
        dests = [d_v[pl.ds(f * xs + x, 1), :] for f in range(fields)]
        zns_v[x] = squeeze([tiles[f * ys] for f in range(fields)], dests)

        @pl.when(sy > 0)
        def _():
            zn_copy(x).start()

    first = interpolate(0)
    send_north(0, first)
    base = fields * xs
    for y in range(ys):
        dests = [d_v[base + f * ys + y : base + f * ys + y + 1, :] for f in range(fields)]
        zes_v[y] = squeeze([first[f * ys + y] for f in range(fields)], dests)

    @pl.when(sx > 0)
    def _():
        ze_copy().start()

    def phase1(x, carry):
        send_north(x, interpolate(x))
        return carry

    lax.fori_loop(1, xs, phase1, 0)

    loads[2].wait()
    for copy in en_loads:
        copy.wait()

    own0 = field * fields

    def phase2(x, carry):
        nxt = jnp.minimum(x + 1, xs - 1)
        for f in range(fields):
            for g in range(fields):
                r = (f * fields + g) * ys
                kt_v[r : r + ys, :] = k_v[f, own0 + g, x]
        kcols = kt_v[...].T
        acols = a_v[x]
        for y in range(ys):
            for f in range(fields):
                r = f * ys + y
                p = [p_v[x, g, y] for g in range(fields)]
                parts = []
                own = mm(w0_v[x, f, y], p[f])
                for g in range(fields):
                    kk = kcols[:, (f * fields + g) * ys + y : (f * fields + g) * ys + y + 1]
                    if g == f:
                        parts.append(((kk + acols[:, r : r + 1]) * p[g].astype(F32) - own).astype(BF))
                    else:
                        parts.append((kk * p[g].astype(F32)).astype(BF))
                parts.append(mm(e_v[f, x, y], p_v[nxt, f, y]).astype(BF))
                if y < ys - 1:
                    parts.append(mm(n_v[f, x, y], p_v[x, f, y + 1]).astype(BF))
                res = mm(q_out[x, f, y], jnp.concatenate(parts, axis=1))
                for g in range(fields):
                    node_out[f, g, x, y] = res[:, g * m : (g + 1) * m].astype(BF)
                east_out[f, x, y] = (-res[:, fields * m : (fields + 1) * m]).astype(BF)
                if y < ys - 1:
                    north_out[f, x, y] = (-res[:, (fields + 1) * m : (fields + 2) * m]).astype(BF)
        return carry

    lax.fori_loop(0, xs, phase2, 0)

    @pl.when(sy < nsy - 1)
    def _():
        d_copy(0).wait_recv()

    @pl.when(sx < nsx - 1)
    def _():
        d_copy(1).wait_recv()

    for y in range(ys):
        for f in range(fields):
            r = base + f * ys + y
            dn_out[r : r + 1, :] = de_v[r : r + 1, :]

    def reorder(tile, dest):
        return mm(tile, one_hot(dest, m, True), NT).astype(BF), mm(tile, one_hot(dest, m, False), NT).astype(BF)

    def phase3(x, carry):
        for f in range(fields):
            a, b = reorder(n_v[f, x, ys - 1], dn_out[pl.ds(f * xs + x, 1), :])
            nef_out[f * xs + x] = a
            nec_out[f * xs + x] = b
        return carry

    lax.fori_loop(0, xs, phase3, 0)
    for f in range(fields):
        for y in range(ys):
            r = base + f * ys + y
            a, b = reorder(e_v[f, xs - 1, y], dn_out[r : r + 1, :])
            nef_out[r] = a
            nec_out[r] = b

    def drain(x, carry):
        p_copy(x).wait()

        @pl.when(sy > 0)
        def _():
            zn_copy(x).wait_send()

        @pl.when(sy < nsy - 1)
        def _():
            zn_copy(x).wait_recv()

        return carry

    lax.fori_loop(0, xs, drain, 0)

    @pl.when(sy > 0)
    def _():
        d_copy(0).wait_send()

    @pl.when(sx > 0)
    def _():
        d_copy(1).wait_send()
        ze_copy().wait_send()

    @pl.when(sx < nsx - 1)
    def _():
        ze_copy().wait_recv()


def finish_kernel(
    counts, q, other, node_own, east_in, north_in, zn, ze, dest, nef, nec, coupling,
    node_out, east_out, north_out,
    k_v, kt_v, node_v, nrim_v, erim_v, k_sem, own_sem, int_sem, cross_sem, rim_sem,
):
    fields, xs, ys, m = counts
    half = m // 2
    field = lax.axis_index("field")
    own0, oth0 = field * fields, (1 - field) * fields
    load = pltpu.make_async_copy(coupling, k_v, k_sem)
    load.start()
    copies = []
    for f in range(fields):
        for g in range(fields):
            copies.append(pltpu.make_async_copy(node_own.at[f, g], node_out.at[f, own0 + g], own_sem.at[f, g]))
    for f in range(fields):
        copies.append(pltpu.make_async_copy(east_in.at[f, : xs - 1], east_out.at[f, : xs - 1], int_sem.at[0, f]))
        for y in range(ys - 1):
            copies.append(pltpu.make_async_copy(north_in.at[f, :, y], north_out.at[f, :, y], int_sem.at[1, f]))
    for copy in copies:
        copy.start()
    load.wait()

    def cross_copy(f, g, x):
        return pltpu.make_async_copy(node_v.at[f, g, x], node_out.at[f, oth0 + g, x], cross_sem.at[f, g, x])

    def cross(x, carry):
        for f in range(fields):
            for g in range(fields):
                r = (f * fields + g) * ys
                kt_v[r : r + ys, :] = k_v[f, oth0 + g, x]
        kcols = kt_v[...].T
        for f in range(fields):
            for y in range(ys):
                parts = []
                for g in range(fields):
                    r = (f * fields + g) * ys + y
                    parts.append((kcols[:, r : r + 1] * other[x, g, y].astype(F32)).astype(BF))
                res = mm(q[x, f, y], jnp.concatenate(parts, axis=1))
                for g in range(fields):
                    node_v[f, g, x, y] = res[:, g * m : (g + 1) * m].astype(BF)
        for f in range(fields):
            for g in range(fields):
                cross_copy(f, g, x).start()
        return carry

    lax.fori_loop(0, xs, cross, 0)

    def rim(z, k, r, d, q_tile):
        zk = z[:, k * half : (k + 1) * half]
        zt = z.T[k * half : (k + 1) * half, :]
        full = jnp.concatenate(
            [jnp.concatenate([zk, zt], axis=1), jnp.concatenate([zt, jnp.zeros_like(zt)], axis=1)], axis=0
        ).astype(BF)
        image = (mm(nef[r], full) + nec[r].astype(F32)).astype(BF)
        packed = (-mm(q_tile, image)).astype(BF)
        return mm(packed, one_hot(d, m, False)).astype(BF)

    def rim_copy(f, x):
        return pltpu.make_async_copy(nrim_v.at[f, x], north_out.at[f, x, ys - 1], rim_sem.at[f, x])

    def north_rim(x, carry):
        z = zn[x].astype(F32)
        for f in range(fields):
            r = f * xs + x
            nrim_v[f, x] = rim(z, f, r, dest[pl.ds(r, 1), :], q[x, f, ys - 1])
        for f in range(fields):
            rim_copy(f, x).start()
        return carry

    lax.fori_loop(0, xs, north_rim, 0)
    base = fields * xs
    last = []
    for y in range(ys):
        z = ze[y].astype(F32)
        for f in range(fields):
            r = base + f * ys + y
            erim_v[f, y] = rim(z, f, r, dest[r : r + 1, :], q[xs - 1, f, y])
    for f in range(fields):
        copy = pltpu.make_async_copy(erim_v.at[f], east_out.at[f, xs - 1], int_sem.at[2, f])
        copy.start()
        last.append(copy)

    def drain(x, carry):
        for f in range(fields):
            rim_copy(f, x).wait()
            for g in range(fields):
                cross_copy(f, g, x).wait()
        return carry

    lax.fori_loop(0, xs, drain, 0)
    for copy in copies + last:
        copy.wait()


def solution(mesh):
    nsx, nsy = mesh.shape["sx"], mesh.shape["sy"]

    def body(inner_block, east_block, north_block, shift_diag, coupling, coarse_flags):
        fields, xs, ys, m = inner_block.shape[:4]
        half = m // 2
        rims = fields * (xs + ys)
        every = coupling.shape[1]
        hbm = pl.BlockSpec(memory_space=pl.ANY)
        vmem = pl.BlockSpec(memory_space=pltpu.VMEM)
        dma = pltpu.SemaphoreType.DMA

        def exchange(*refs):
            exchange_kernel((nsx, nsy, fields, xs, ys, m), *refs)

        def finish(*refs):
            finish_kernel((fields, xs, ys, m), *refs)

        mid = pl.pallas_call(
            exchange,
            out_shape=[
                pltpu.VMEM((xs, fields, ys, m, m), BF),
                pltpu.VMEM((xs, fields, ys, m, m), BF),
                pltpu.VMEM((fields, fields, xs, ys, m, m), BF),
                pltpu.VMEM((fields, xs, ys, m, m), BF),
                pltpu.VMEM((fields, xs, ys, m, m), BF),
                pltpu.VMEM((xs, half, m), BF),
                pltpu.VMEM((ys, half, m), BF),
                pltpu.VMEM((rims, m), F32),
                pltpu.VMEM((rims, m, m), BF),
                pltpu.VMEM((rims, m, m), BF),
            ],
            in_specs=[hbm] * 6,
            out_specs=[vmem] * 10,
            scratch_shapes=[
                pltpu.VMEM((fields, xs, ys, m, m), BF),
                pltpu.VMEM((fields, xs, ys, m, m), BF),
                pltpu.VMEM((fields, xs, ys, m, m), BF),
                pltpu.VMEM((fields, xs, ys, m), F32),
                pltpu.VMEM((fields, every, xs, ys, m), F32),
                pltpu.VMEM((fields, xs, ys, m), jnp.int32),
                pltpu.VMEM((xs, fields, ys, m, m), BF),
                pltpu.VMEM((xs, fields, ys, m, m), BF),
                pltpu.VMEM((xs, m, fields * ys), F32),
                pltpu.VMEM((rims, m), F32),
                pltpu.VMEM((rims, m), F32),
                pltpu.VMEM((xs, half, m), BF),
                pltpu.VMEM((ys, half, m), BF),
                pltpu.VMEM((rims, m), F32),
                pltpu.VMEM((8, m), F32),
                pltpu.VMEM((8, m), F32),
                dma((fields, xs)), dma((3,)), dma((2,)),
                dma((xs,)), dma((xs,)), dma(()), dma(()), dma((2,)), dma((2,)), dma((xs,)), dma((xs,)),
            ],
            compiler_params=pltpu.CompilerParams(
                collective_id=0, has_side_effects=True, vmem_limit_bytes=24 * MIB
            ),
            name="exchange",
        )(inner_block, east_block, north_block, shift_diag, coupling, coarse_flags)

        return pl.pallas_call(
            finish,
            out_shape=[
                jax.ShapeDtypeStruct((fields, every, xs, ys, m, m), BF),
                jax.ShapeDtypeStruct((fields, xs, ys, m, m), BF),
                jax.ShapeDtypeStruct((fields, xs, ys, m, m), BF),
            ],
            in_specs=[vmem] * 10 + [hbm],
            out_specs=[hbm] * 3,
            scratch_shapes=[
                pltpu.VMEM((fields, every, xs, ys, m), F32),
                pltpu.VMEM((8, m), F32),
                pltpu.VMEM((fields, fields, xs, ys, m, m), BF),
                pltpu.VMEM((fields, xs, m, m), BF),
                pltpu.VMEM((fields, ys, m, m), BF),
                dma(()), dma((fields, fields)), dma((3, fields)), dma((fields, fields, xs)), dma((fields, xs)),
            ],
            compiler_params=pltpu.CompilerParams(vmem_limit_bytes=24 * MIB),
            name="finish",
        )(*mid, coupling)

    in_specs = (
        P("field", "sx", "sy", None, None),
        P("field", "sx", "sy", None, None),
        P("field", "sx", "sy", None, None),
        P("field", "sx", "sy", None),
        P("field", None, "sx", "sy", None),
        P("field", "sx", "sy", None),
    )
    out_specs = (
        P("field", None, "sx", "sy", None, None),
        P("field", "sx", "sy", None, None),
        P("field", "sx", "sy", None, None),
    )
    return jax.shard_map(body, mesh=mesh, in_specs=in_specs, out_specs=out_specs, check_vma=False)
```

```python
import jax
import jax.numpy as jnp
from jax import lax
from jax.experimental import pallas as pl
from jax.experimental.pallas import tpu as pltpu
from jax.sharding import PartitionSpec as P

BF = jnp.bfloat16
F32 = jnp.float32
MESH = pl.DeviceIdType.MESH
NN = (((1,), (0,)), ((), ()))
NT = (((1,), (1,)), ((), ()))
MIB = 1 << 20
PAD = 24


def mm(left, right, dims=NN):
    return lax.dot_general(left, right, dims, preferred_element_type=F32)


def iota(shape, axis):
    return lax.broadcasted_iota(jnp.int32, shape, axis)


def fine_hot(dest, m):
    return jnp.where(-1.0 - dest == iota((m, m), 0).astype(F32), 1.0, 0.0).astype(BF)


def coarse_hot(dest, m):
    return jnp.where(dest == iota((m, m), 0).astype(F32), 1.0, 0.0).astype(BF)


def exchange_kernel(
    dims, inner, east, north, shift, coupling, flags,
    q_out, other_out, node_out, east_out, north_out, zn_out, ze_out, dn_out, de_out, ne_out, kt_out,
    w_v, e_v, n_v, s_v, k_v, c_v, p_v, w0_v, wt_v, c_r, s_r, a_r, tot_r, str_r, k_r, fac_t, d_v, y_v, x_v,
    zns_v, zes_v, eye_v, off_v,
    w_sem, vec_sem, en_sem, zs_sem, zr_sem, es_sem, er_sem, ds_sem, dr_sem, ps_sem, pr_sem,
):
    nsx, nsy, fields, xs, ys, m = dims
    half = m // 2
    tiles = [(x, f) for x in range(xs) for f in range(fields)]
    field, sx, sy = lax.axis_index("field"), lax.axis_index("sx"), lax.axis_index("sy")
    barrier = pltpu.get_barrier_semaphore()
    partner = {"field": 1 - field}

    flag_load = pltpu.make_async_copy(flags, c_v, vec_sem.at[0])
    shift_load = pltpu.make_async_copy(shift, s_v, vec_sem.at[1])
    k_load = pltpu.make_async_copy(coupling, k_v, vec_sem.at[2])
    w_loads = [pltpu.make_async_copy(inner.at[:, :, y], w_v.at[y], w_sem.at[y]) for y in range(ys)]
    e_load = pltpu.make_async_copy(east, e_v, en_sem.at[0])
    n_load = pltpu.make_async_copy(north, n_v, en_sem.at[1])
    flag_load.start()
    w_loads[0].start()
    shift_load.start()
    for copy in w_loads[1:]:
        copy.start()

    pl.semaphore_signal(barrier, inc=1, device_id=partner, device_id_type=MESH)

    @pl.when(sy < nsy - 1)
    def _():
        pl.semaphore_signal(barrier, inc=1, device_id={"sy": sy + 1}, device_id_type=MESH)

    @pl.when(sx < nsx - 1)
    def _():
        pl.semaphore_signal(barrier, inc=1, device_id={"sx": sx + 1}, device_id_type=MESH)

    k_load.start()
    e_load.start()
    n_load.start()

    unit = iota((m, m), 0) == iota((m, m), 1)
    eye_v[...] = jnp.where(unit, 1.0, 0.0).astype(BF)
    off_v[...] = jnp.where(unit, 0.0, 1.0).astype(BF)

    c_r[...] = jnp.zeros(c_r.shape, F32)
    s_r[...] = jnp.ones(s_r.shape, F32)
    k_r[...] = jnp.zeros(k_r.shape, F32)
    tot_r[...] = jnp.ones(tot_r.shape, F32)
    str_r[...] = jnp.ones(str_r.shape, F32)
    flag_load.wait()
    for t, (x, f) in enumerate(tiles):
        row = c_v[f, x].astype(F32)
        for y in range(ys):
            c_r[y, t : t + 1, :] = row[y : y + 1, :]
    before = jnp.where(iota((m, m), 0) < iota((m, m), 1), 1.0, 0.0).astype(BF)
    for y in range(ys):
        c = c_r[y]
        rank_c = mm(c.astype(BF), before)
        count = jnp.sum(c, axis=1, keepdims=True)
        short = jnp.minimum(count, m - count)
        rank = jnp.where(c > 0.5, rank_c, iota((PAD, m), 1).astype(F32) - rank_c)
        place = jnp.where(rank < half, rank, rank + short)
        d_v[y] = jnp.where(c > 0.5, place, -1.0 - place)

    pl.semaphore_wait(barrier, 1 + jnp.where(sy > 0, 1, 0) + jnp.where(sx > 0, 1, 0))

    def to_north(src, dst, send, recv):
        return pltpu.make_async_remote_copy(
            src_ref=src, dst_ref=dst, send_sem=send, recv_sem=recv, device_id={"sy": sy - 1}, device_id_type=MESH)

    def to_east(src, dst, send, recv):
        return pltpu.make_async_remote_copy(
            src_ref=src, dst_ref=dst, send_sem=send, recv_sem=recv, device_id={"sx": sx - 1}, device_id_type=MESH)

    dn_copy = to_north(d_v.at[0], dn_out, ds_sem.at[0], dr_sem.at[0])
    de_copy = to_east(d_v.at[:, 0:8], de_out, ds_sem.at[1], dr_sem.at[1])
    zn_copies = [to_north(zns_v.at[x], zn_out.at[x], zs_sem.at[x], zr_sem.at[x]) for x in range(xs)]
    ze_copies = [
        to_east(zns_v.at[0] if y == 0 else zes_v.at[y], ze_out.at[y], es_sem.at[y], er_sem.at[y]) for y in range(ys)
    ]
    p_copies = [
        pltpu.make_async_remote_copy(
            src_ref=p_v.at[y], dst_ref=other_out.at[y], send_sem=ps_sem.at[y], recv_sem=pr_sem.at[y],
            device_id=partner, device_id_type=MESH)
        for y in range(ys)
    ]

    @pl.when(sy > 0)
    def _():
        dn_copy.start()

    @pl.when(sx > 0)
    def _():
        de_copy.start()

    @pl.when(sy == nsy - 1)
    def _():
        dn_out[...] = jnp.full(dn_out.shape, -1.0, F32)
        zn_out[...] = jnp.zeros(zn_out.shape, BF)

    @pl.when(sx == nsx - 1)
    def _():
        de_out[...] = jnp.full(de_out.shape, -1.0, F32)
        ze_out[...] = jnp.zeros(ze_out.shape, BF)

    shift_load.wait()
    for t, (x, f) in enumerate(tiles):
        row = s_v[f, x]
        for y in range(ys):
            s_r[y, t : t + 1, :] = row[y : y + 1, :]

    def interpolate(y):
        for x in range(xs):
            left = jnp.concatenate(
                [jnp.ones((1, m), F32), c_r[y, x * fields : (x + 1) * fields, :], jnp.zeros((15 - fields, m), F32)], axis=0
            ).astype(BF)
            for f in range(fields):
                t = x * fields + f
                w0 = w_v[y, f, x] * off_v[...]
                w0_v[y, x, f] = w0
                sums = mm(left, w0, NT)
                tot_r[y, t : t + 1, :] = sums[0:1, :]
                str_r[y, t : t + 1, :] = sums[1 + f : 2 + f, :]
        total, c = tot_r[y], c_r[y]
        diag = total + s_r[y]
        alpha = total / jnp.maximum(str_r[y], total * (1.0 / 32.0))
        factor = (1.0 - c) * alpha / diag
        a_r[y] = diag
        fac_t[y] = jnp.concatenate([factor, jnp.zeros((m - PAD, m), F32)], axis=0).T
        for t, (x, f) in enumerate(tiles):
            chosen = jnp.broadcast_to(c_r[y, t : t + 1, :], (m, m)).astype(BF)
            scaled = (fac_t[y, :, t : t + 1] * w0_v[y, x, f].astype(F32)).astype(BF)
            p_v[y, x, f] = scaled * chosen + eye_v[...] * chosen

    def squeeze(y, some):
        for x, f in some:
            t = x * fields + f
            y_v[y, t] = mm(fine_hot(d_v[y, t : t + 1, :], m), p_v[y, x, f]).astype(BF)
        for x, f in some:
            t = x * fields + f
            x_v[y, t] = mm(y_v[y, t], coarse_hot(d_v[y, t : t + 1, :], m), NT).astype(BF)

    def folded(y, x):
        parts = []
        for f in range(fields):
            t = x * fields + f
            turned = x_v[y, t].T
            parts.append(x_v[y, t, :half, :half] + turned[:half, half:] + turned[half:, :half])
        return jnp.concatenate(parts, axis=1)

    w_loads[0].wait()
    interpolate(0)
    squeeze(0, tiles)
    for x in range(xs):
        zns_v[x] = folded(0, x)

        @pl.when(sy > 0)
        def _():
            zn_copies[x].start()

    @pl.when(sx > 0)
    def _():
        ze_copies[0].start()

    p_copies[0].start()
    for y in range(1, ys):
        w_loads[y].wait()
        interpolate(y)
        squeeze(y, tiles[:fields])
        zes_v[y] = folded(y, 0)

        @pl.when(sx > 0)
        def _():
            ze_copies[y].start()

        p_copies[y].start()

    for y in range(ys):
        for x, f in tiles:
            q_out[y, x, f] = p_v[y, x, f].T

    k_load.wait()
    own0, oth0 = field * fields, (1 - field) * fields
    for t, (x, f) in enumerate(tiles):
        rows = [k_v[f, own0 + f, x], k_v[f, own0 + (1 - f), x], k_v[f, oth0, x], k_v[f, oth0 + 1, x]]
        for j, row in enumerate(rows):
            for y in range(ys):
                k_r[y, j * PAD + t : j * PAD + t + 1, :] = row[y : y + 1, :]
    for y in range(ys):
        k_r[y, :PAD, :] = k_r[y, :PAD, :] + a_r[y]
        kt_out[y] = k_r[y].T

    e_load.wait()
    n_load.wait()

    def column(j, y, t):
        return kt_out[y, :, j * PAD + t : j * PAD + t + 1]

    for y in range(ys):
        for t, (x, f) in enumerate(tiles):
            p = p_v[y, x, f]
            own = mm(w0_v[y, x, f], p)
            wt_v[y, x, f, :, f * m : (f + 1) * m] = (column(0, y, t) * p.astype(F32) - own).astype(BF)
            wt_v[y, x, f, :, (1 - f) * m : (2 - f) * m] = (column(1, y, t) * p_v[y, x, 1 - f].astype(F32)).astype(BF)
            if x < xs - 1:
                wt_v[y, x, f, :, 2 * m : 3 * m] = mm(e_v[f, x, y], p_v[y, x + 1, f]).astype(BF)
            if y < ys - 1:
                wt_v[y, x, f, :, 3 * m : 4 * m] = mm(n_v[f, x, y], p_v[y + 1, x, f]).astype(BF)
    for y in range(ys):
        for x, f in tiles:
            q = q_out[y, x, f]
            res = mm(q, wt_v[y, x, f, :, : 2 * m])
            for g in range(fields):
                node_out[f, g, x, y] = res[:, g * m : (g + 1) * m].astype(BF)
            if x < xs - 1:
                east_out[f, x, y] = (-mm(q, wt_v[y, x, f, :, 2 * m : 3 * m])).astype(BF)
            if y < ys - 1:
                north_out[f, x, y] = (-mm(q, wt_v[y, x, f, :, 3 * m : 4 * m])).astype(BF)

    @pl.when(sy < nsy - 1)
    def _():
        dn_copy.wait_recv()

    @pl.when(sx < nsx - 1)
    def _():
        de_copy.wait_recv()

    def reorder(tile, dest):
        return mm(tile, jnp.concatenate([fine_hot(dest, m), coarse_hot(dest, m)], axis=0), NT).astype(BF)

    for t, (x, f) in enumerate(tiles):
        ne_out[t] = reorder(n_v[f, x, ys - 1], dn_out[t : t + 1, :])
    for y in range(ys):
        for f in range(fields):
            ne_out[len(tiles) + y * fields + f] = reorder(e_v[f, xs - 1, y], de_out[y, f : f + 1, :])

    @pl.when(sy > 0)
    def _():
        dn_copy.wait_send()
        for copy in zn_copies:
            copy.wait_send()

    @pl.when(sx > 0)
    def _():
        de_copy.wait_send()
        for copy in ze_copies:
            copy.wait_send()

    for copy in p_copies:
        copy.wait()

    @pl.when(sx < nsx - 1)
    def _():
        for copy in ze_copies:
            copy.wait_recv()

    @pl.when(sy < nsy - 1)
    def _():
        for copy in zn_copies:
            copy.wait_recv()


def finish_kernel(
    dims, q, other, node_own, east_in, north_in, zn, ze, dn, de, ne, kt,
    node_out, east_out, north_out,
    wt_v, node_v, full_v, im_v, pk_v, nrim_v, erim_v, own_sem, int_sem, cross_sem, rim_sem,
):
    fields, xs, ys, m = dims
    half = m // 2
    tiles = [(x, f) for x in range(xs) for f in range(fields)]
    field = lax.axis_index("field")
    own0, oth0 = field * fields, (1 - field) * fields
    copies = []

    def put(src, dst, sem):
        copy = pltpu.make_async_copy(src, dst, sem)
        copy.start()
        copies.append(copy)

    for f in range(fields):
        for g in range(fields):
            put(node_own.at[f, g], node_out.at[f, own0 + g], own_sem.at[f, g])
    for f in range(fields):
        put(east_in.at[f, : xs - 1], east_out.at[f, : xs - 1], int_sem.at[0, f])
        put(north_in.at[f, :, 0], north_out.at[f, :, 0], int_sem.at[1, f])

    def column(j, y, t):
        return kt[y, :, j * PAD + t : j * PAD + t + 1]

    for y in range(ys):
        for t, (x, f) in enumerate(tiles):
            for g in range(fields):
                wt_v[y, x, f, :, g * m : (g + 1) * m] = (column(2 + g, y, t) * other[y, x, g].astype(F32)).astype(BF)
    for x in range(xs):
        for f in range(fields):
            for y in range(ys):
                res = mm(q[y, x, f], wt_v[y, x, f])
                for g in range(fields):
                    node_v[f, g, x, y] = res[:, g * m : (g + 1) * m].astype(BF)
            for g in range(fields):
                put(node_v.at[f, g, x], node_out.at[f, oth0 + g, x], cross_sem.at[f, g, x])

    rims = []
    for t, (x, f) in enumerate(tiles):
        rims.append((zn, x, f, q.at[ys - 1, x, f], dn.at[t : t + 1, :]))
    for y in range(ys):
        for f in range(fields):
            rims.append((ze, y, f, q.at[y, xs - 1, f], de.at[y, f : f + 1, :]))
    for r, (z, i, f, _, _) in enumerate(rims):
        turned = z[i].T[f * half : (f + 1) * half, :]
        full_v[r, :half, :half] = z[i, :, f * half : (f + 1) * half]
        full_v[r, half:, :half] = turned
        full_v[r, :half, half:] = turned
        full_v[r, half:, half:] = jnp.zeros((half, half), BF)
    for r in range(len(rims)):
        im_v[r] = (mm(ne[r, :, :m], full_v[r]) + ne[r, :, m:].astype(F32)).astype(BF)
    for r, (_, _, _, tile, _) in enumerate(rims):
        pk_v[r] = (-mm(tile[...], im_v[r])).astype(BF)
    for t, (x, f) in enumerate(tiles):
        nrim_v[f, x] = mm(pk_v[t], coarse_hot(rims[t][4][...], m)).astype(BF)
    for f in range(fields):
        put(nrim_v.at[f], north_out.at[f, :, ys - 1], rim_sem.at[0, f])
    for y in range(ys):
        for f in range(fields):
            r = len(tiles) + y * fields + f
            erim_v[f, y] = mm(pk_v[r], coarse_hot(rims[r][4][...], m)).astype(BF)
    for f in range(fields):
        put(erim_v.at[f], east_out.at[f, xs - 1], rim_sem.at[1, f])
    for copy in copies:
        copy.wait()


def solution(mesh):
    nsx, nsy = mesh.shape["sx"], mesh.shape["sy"]

    def body(inner_block, east_block, north_block, shift_diag, coupling, coarse_flags):
        fields, xs, ys, m = inner_block.shape[:4]
        half = m // 2
        rims = fields * (xs + ys)
        every = coupling.shape[1]
        hbm = pl.BlockSpec(memory_space=pltpu.HBM)
        vmem = pl.BlockSpec(memory_space=pltpu.VMEM)
        dma = pltpu.SemaphoreType.DMA

        def exchange(*refs):
            exchange_kernel((nsx, nsy, fields, xs, ys, m), *refs)

        def finish(*refs):
            finish_kernel((fields, xs, ys, m), *refs)

        mid = pl.pallas_call(
            exchange,
            out_shape=[
                pltpu.VMEM((ys, xs, fields, m, m), BF),
                pltpu.VMEM((ys, xs, fields, m, m), BF),
                pltpu.VMEM((fields, fields, xs, ys, m, m), BF),
                pltpu.VMEM((fields, xs, ys, m, m), BF),
                pltpu.VMEM((fields, xs, ys, m, m), BF),
                pltpu.VMEM((xs, half, m), BF),
                pltpu.VMEM((ys, half, m), BF),
                pltpu.VMEM((PAD, m), F32),
                pltpu.VMEM((ys, 8, m), F32),
                pltpu.VMEM((rims, m, 2 * m), BF),
                pltpu.VMEM((ys, m, m), F32),
            ],
            in_specs=[hbm] * 6,
            out_specs=[vmem] * 11,
            scratch_shapes=[
                pltpu.VMEM((ys, fields, xs, m, m), BF),
                pltpu.VMEM((fields, xs, ys, m, m), BF),
                pltpu.VMEM((fields, xs, ys, m, m), BF),
                pltpu.VMEM((fields, xs, ys, m), F32),
                pltpu.VMEM((fields, every, xs, ys, m), F32),
                pltpu.VMEM((fields, xs, ys, m), jnp.int32),
                pltpu.VMEM((ys, xs, fields, m, m), BF),
                pltpu.VMEM((ys, xs, fields, m, m), BF),
                pltpu.VMEM((ys, xs, fields, m, 4 * m), BF),
                pltpu.VMEM((ys, PAD, m), F32),
                pltpu.VMEM((ys, PAD, m), F32),
                pltpu.VMEM((ys, PAD, m), F32),
                pltpu.VMEM((ys, PAD, m), F32),
                pltpu.VMEM((ys, PAD, m), F32),
                pltpu.VMEM((ys, m, m), F32),
                pltpu.VMEM((ys, m, m), F32),
                pltpu.VMEM((ys, PAD, m), F32),
                pltpu.VMEM((ys, PAD, m, m), BF),
                pltpu.VMEM((ys, PAD, m, m), BF),
                pltpu.VMEM((xs, half, m), BF),
                pltpu.VMEM((ys, half, m), BF),
                pltpu.VMEM((m, m), BF),
                pltpu.VMEM((m, m), BF),
                dma((ys,)), dma((3,)), dma((2,)),
                dma((xs,)), dma((xs,)), dma((ys,)), dma((ys,)), dma((2,)), dma((2,)), dma((ys,)), dma((ys,)),
            ],
            compiler_params=pltpu.CompilerParams(
                collective_id=0, has_side_effects=True, vmem_limit_bytes=32 * MIB
            ),
            name="exchange",
        )(*[
            pltpu.with_memory_space_constraint(a, pltpu.HBM)
            for a in (inner_block, east_block, north_block, shift_diag, coupling, coarse_flags)
        ])

        return pl.pallas_call(
            finish,
            out_shape=[
                jax.ShapeDtypeStruct((fields, every, xs, ys, m, m), BF),
                jax.ShapeDtypeStruct((fields, xs, ys, m, m), BF),
                jax.ShapeDtypeStruct((fields, xs, ys, m, m), BF),
            ],
            in_specs=[vmem] * 11,
            out_specs=[hbm] * 3,
            scratch_shapes=[
                pltpu.VMEM((ys, xs, fields, m, 2 * m), BF),
                pltpu.VMEM((fields, fields, xs, ys, m, m), BF),
                pltpu.VMEM((rims, m, m), BF),
                pltpu.VMEM((rims, m, m), BF),
                pltpu.VMEM((rims, m, m), BF),
                pltpu.VMEM((fields, xs, m, m), BF),
                pltpu.VMEM((fields, ys, m, m), BF),
                dma((fields, fields)), dma((2, fields)), dma((fields, fields, xs)), dma((2, fields)),
            ],
            compiler_params=pltpu.CompilerParams(vmem_limit_bytes=24 * MIB),
            name="finish",
        )(*mid)

    in_specs = (
        P("field", "sx", "sy", None, None),
        P("field", "sx", "sy", None, None),
        P("field", "sx", "sy", None, None),
        P("field", "sx", "sy", None),
        P("field", None, "sx", "sy", None),
        P("field", "sx", "sy", None),
    )
    out_specs = (
        P("field", None, "sx", "sy", None, None),
        P("field", "sx", "sy", None, None),
        P("field", "sx", "sy", None, None),
    )
    return jax.shard_map(body, mesh=mesh, in_specs=in_specs, out_specs=out_specs, check_vma=False)
```

```python
import jax
import jax.numpy as jnp
from jax import lax
from jax.experimental import pallas as pl
from jax.experimental.pallas import tpu as pltpu
from jax.sharding import PartitionSpec as P

BF = jnp.bfloat16
F32 = jnp.float32
MESH = pl.DeviceIdType.MESH
NN = (((1,), (0,)), ((), ()))
NT = (((1,), (1,)), ((), ()))
MIB = 1 << 20
PAD = 24


def mm(left, right, dims=NN):
    return lax.dot_general(left, right, dims, preferred_element_type=F32)


def iota(shape, axis):
    return lax.broadcasted_iota(jnp.int32, shape, axis)


def fine_hot(dest, m):
    return jnp.where(-1.0 - dest == iota((m, m), 0).astype(F32), 1.0, 0.0).astype(BF)


def coarse_hot(dest, m):
    return jnp.where(dest == iota((m, m), 0).astype(F32), 1.0, 0.0).astype(BF)


def exchange_kernel(
    dims, inner, east, north, shift, coupling, flags,
    q_out, cross_out, node_out, east_out, north_out, zn_out, ze_out, dn_out, de_out, ne_out,
    w_v, e_v, n_v, s_v, k_v, c_v, p_v, w0_v, wt_v, c_r, s_r, a_r, tot_r, str_r, k_r, fac_t, d_v, y_v, x_v,
    zns_v, zes_v, eye_v, off_v, dnr_v, der_v, other_v, wo_v, kt_v,
    w_sem, vec_sem, en_sem, zs_sem, zr_sem, es_sem, er_sem, ds_sem, dr_sem, ps_sem, pr_sem,
):
    nsx, nsy, fields, xs, ys, m = dims
    half = m // 2
    tiles = [(x, f) for x in range(xs) for f in range(fields)]
    step = -(-xs // 2)
    groups = [(a, min(a + step, xs)) for a in range(0, xs, step)]
    field, sx, sy = lax.axis_index("field"), lax.axis_index("sx"), lax.axis_index("sy")
    barrier = pltpu.get_barrier_semaphore()
    partner = {"field": 1 - field}

    flag_load = pltpu.make_async_copy(flags, c_v, vec_sem.at[0])
    shift_load = pltpu.make_async_copy(shift, s_v, vec_sem.at[1])
    k_load = pltpu.make_async_copy(coupling, k_v, vec_sem.at[2])
    w_loads = [pltpu.make_async_copy(inner.at[:, :, y], w_v.at[y], w_sem.at[y]) for y in range(ys)]
    e_load = pltpu.make_async_copy(east, e_v, en_sem.at[0])
    n_load = pltpu.make_async_copy(north, n_v, en_sem.at[1])
    flag_load.start()
    w_loads[0].start()

    pl.semaphore_signal(barrier, inc=1, device_id=partner, device_id_type=MESH)


    @pl.when(sy < nsy - 1)
    def _():
        pl.semaphore_signal(barrier, inc=1, device_id={"sy": sy + 1}, device_id_type=MESH)

    pl.semaphore_signal(barrier, inc=1, device_id={"sx": lax.rem(sx + 1, nsx)}, device_id_type=MESH)

    unit = iota((m, m), 0) == iota((m, m), 1)
    eye_v[...] = jnp.where(unit, 1.0, 0.0).astype(BF)
    off_v[...] = jnp.where(unit, 0.0, 1.0).astype(BF)

    c_r[...] = jnp.zeros(c_r.shape, F32)
    s_r[...] = jnp.ones(s_r.shape, F32)
    k_r[...] = jnp.zeros(k_r.shape, F32)
    tot_r[...] = jnp.ones(tot_r.shape, F32)
    str_r[...] = jnp.ones(str_r.shape, F32)
    flag_load.wait()
    for t, (x, f) in enumerate(tiles):
        row = c_v[f, x].astype(F32)
        for y in range(ys):
            c_r[y, t : t + 1, :] = row[y : y + 1, :]
    before = jnp.where(iota((m, m), 0) < iota((m, m), 1), 1.0, 0.0).astype(BF)
    for y in range(ys):
        c = c_r[y]
        rank_c = mm(c.astype(BF), before)
        count = jnp.sum(c, axis=1, keepdims=True)
        short = jnp.minimum(count, m - count)
        rank = jnp.where(c > 0.5, rank_c, iota((PAD, m), 1).astype(F32) - rank_c)
        place = jnp.where(rank < half, rank, rank + short)
        d_v[y] = jnp.where(c > 0.5, place, -1.0 - place)


    def to_north(src, dst, send, recv):
        return pltpu.make_async_remote_copy(
            src_ref=src, dst_ref=dst, send_sem=send, recv_sem=recv, device_id={"sy": sy - 1}, device_id_type=MESH)

    def to_east(src, dst, send, recv):
        return pltpu.make_async_remote_copy(
            src_ref=src, dst_ref=dst, send_sem=send, recv_sem=recv, device_id={"sx": lax.rem(sx + nsx - 1, nsx)}, device_id_type=MESH)

    dn_copy = to_north(d_v.at[0], dnr_v, ds_sem.at[0], dr_sem.at[0])
    de_copy = to_east(d_v.at[:, 0:8], der_v, ds_sem.at[1], dr_sem.at[1])
    zn_copies = [to_north(zns_v.at[a:b], zn_out.at[a:b], zs_sem.at[k], zr_sem.at[k]) for k, (a, b) in enumerate(groups)]
    ze_copies = [
        to_east(zns_v.at[0] if y == 0 else zes_v.at[y], ze_out.at[y], es_sem.at[y], er_sem.at[y]) for y in range(ys)
    ]
    p_copies = [
        pltpu.make_async_remote_copy(
            src_ref=p_v.at[y], dst_ref=other_v.at[y], send_sem=ps_sem.at[y], recv_sem=pr_sem.at[y],
            device_id=partner, device_id_type=MESH)
        for y in range(ys)
    ]

    @pl.when(sy == nsy - 1)
    def _():
        dnr_v[...] = jnp.zeros(dnr_v.shape, F32)
        zn_out[...] = jnp.zeros(zn_out.shape, BF)


    def interpolate(y):
        for x in range(xs):
            left = jnp.concatenate(
                [jnp.ones((1, m), F32), c_r[y, x * fields : (x + 1) * fields, :], jnp.zeros((15 - fields, m), F32)], axis=0
            ).astype(BF)
            for f in range(fields):
                t = x * fields + f
                w0 = w_v[y, f, x] * off_v[...]
                w0_v[y, x, f] = w0
                sums = mm(left, w0, NT)
                tot_r[y, t : t + 1, :] = sums[0:1, :]
                str_r[y, t : t + 1, :] = sums[1 + f : 2 + f, :]
        total, c = tot_r[y], c_r[y]
        diag = total + s_r[y]
        alpha = total / jnp.maximum(str_r[y], total * (1.0 / 32.0))
        factor = (1.0 - c) * alpha / diag
        a_r[y] = diag
        fac_t[y] = jnp.concatenate([factor, jnp.zeros((m - PAD, m), F32)], axis=0).T
        for t, (x, f) in enumerate(tiles):
            chosen = jnp.broadcast_to(c_r[y, t : t + 1, :], (m, m)).astype(BF)
            scaled = (fac_t[y, :, t : t + 1] * w0_v[y, x, f].astype(F32)).astype(BF)
            p_v[y, x, f] = scaled * chosen + eye_v[...] * chosen

    def squeeze(y, some):
        for x, f in some:
            t = x * fields + f
            y_v[y, t] = mm(fine_hot(d_v[y, t : t + 1, :], m), p_v[y, x, f]).astype(BF)
        for x, f in some:
            t = x * fields + f
            x_v[y, t] = mm(y_v[y, t], coarse_hot(d_v[y, t : t + 1, :], m), NT).astype(BF)

    def folded(y, x):
        parts = []
        for f in range(fields):
            t = x * fields + f
            turned = x_v[y, t].T
            parts.append(x_v[y, t, :half, :half] + turned[:half, half:] + turned[half:, :half])
        return jnp.concatenate(parts, axis=1)

    prompt = sy != nsy // 2
    w_loads[0].wait()
    shift_load.start()
    for copy in w_loads[1:]:
        copy.start()
    k_load.start()
    e_load.start()
    n_load.start()
    shift_load.wait()
    for t, (x, f) in enumerate(tiles):
        row = s_v[f, x]
        for y in range(ys):
            s_r[y, t : t + 1, :] = row[y : y + 1, :]
    interpolate(0)
    for k, (a, b) in enumerate(groups):
        squeeze(0, tiles[a * fields : b * fields])
        for x in range(a, b):
            zns_v[x] = folded(0, x)

        if k == 0:
            @pl.when(prompt)
            def _():
                pl.semaphore_wait(barrier, jnp.where(sy > 0, 3, 2))

        @pl.when(prompt & (sy > 0))
        def _():
            if k == 0:
                dn_copy.start()
            zn_copies[k].start()

    @pl.when(prompt)
    def _():
        for copy in [de_copy, ze_copies[0], p_copies[0]]:
            copy.start()

    for y in range(1, ys):
        w_loads[y].wait()
        interpolate(y)
        squeeze(y, tiles[:fields])
        zes_v[y] = folded(y, 0)

    @pl.when(prompt)
    def _():
        for copy in ze_copies[1:] + p_copies[1:]:
            copy.start()

    for y in range(ys):
        for x, f in tiles:
            q_out[y, x, f] = p_v[y, x, f].T

    k_load.wait()
    own0, oth0 = field * fields, (1 - field) * fields
    for t, (x, f) in enumerate(tiles):
        rows = [k_v[f, own0 + f, x], k_v[f, own0 + (1 - f), x], k_v[f, oth0, x], k_v[f, oth0 + 1, x]]
        for j, row in enumerate(rows):
            for y in range(ys):
                k_r[y, j * PAD + t : j * PAD + t + 1, :] = row[y : y + 1, :]
    for y in range(ys):
        k_r[y, :PAD, :] = k_r[y, :PAD, :] + a_r[y]
        kt_v[y] = k_r[y].T

    @pl.when(jnp.logical_not(prompt))
    def _():
        pl.semaphore_wait(barrier, 3)
        for copy in [dn_copy, de_copy] + zn_copies + ze_copies + p_copies:
            copy.start()

    e_load.wait()
    n_load.wait()

    def column(j, y, t):
        return kt_v[y, :, j * PAD + t : j * PAD + t + 1]

    for y in range(ys):
        for t, (x, f) in enumerate(tiles):
            p = p_v[y, x, f]
            own = mm(w0_v[y, x, f], p)
            wt_v[y, x, f, :, f * m : (f + 1) * m] = (column(0, y, t) * p.astype(F32) - own).astype(BF)
            wt_v[y, x, f, :, (1 - f) * m : (2 - f) * m] = (column(1, y, t) * p_v[y, x, 1 - f].astype(F32)).astype(BF)
            if x < xs - 1:
                wt_v[y, x, f, :, 2 * m : 3 * m] = mm(e_v[f, x, y], p_v[y, x + 1, f]).astype(BF)
            if y < ys - 1:
                wt_v[y, x, f, :, 3 * m : 4 * m] = mm(n_v[f, x, y], p_v[y + 1, x, f]).astype(BF)
    for y in range(ys):
        for x, f in tiles:
            q = q_out[y, x, f]
            res = mm(q, wt_v[y, x, f, :, : 2 * m])
            for g in range(fields):
                node_out[f, g, x, y] = res[:, g * m : (g + 1) * m].astype(BF)
            if x < xs - 1:
                east_out[f, x, y] = (-mm(q, wt_v[y, x, f, :, 2 * m : 3 * m])).astype(BF)
            if y < ys - 1:
                north_out[f, x, y] = (-mm(q, wt_v[y, x, f, :, 3 * m : 4 * m])).astype(BF)

    @pl.when(sy < nsy - 1)
    def _():
        dn_copy.wait_recv()

    de_copy.wait()
    dn_out[...] = jnp.where(sy < nsy - 1, dnr_v[...], m * 4.0)
    de_out[...] = jnp.where(sx < nsx - 1, der_v[...], m * 4.0)

    def reorder(r, tile, dest):
        ne_out[r] = mm(tile, jnp.concatenate([fine_hot(dest, m), coarse_hot(dest, m)], axis=0), NT).astype(BF)

    for t, (x, f) in enumerate(tiles):
        reorder(t, n_v[f, x, ys - 1], dn_out[t : t + 1, :])
    for y in range(ys):
        for f in range(fields):
            reorder(len(tiles) + y * fields + f, e_v[f, xs - 1, y], de_out[y, f : f + 1, :])

    for copy in p_copies:
        copy.wait()
    for y in range(ys):
        for t, (x, f) in enumerate(tiles):
            for g in range(fields):
                wo_v[y, x, f, :, g * m : (g + 1) * m] = (column(2 + g, y, t) * other_v[y, x, g].astype(F32)).astype(BF)
    for y in range(ys):
        for x, f in tiles:
            res = mm(q_out[y, x, f], wo_v[y, x, f])
            for g in range(fields):
                cross_out[f, g, x, y] = res[:, g * m : (g + 1) * m].astype(BF)

    for copy in ze_copies:
        copy.wait()

    @pl.when(sy > 0)
    def _():
        for copy in [dn_copy] + zn_copies:
            copy.wait_send()

    @pl.when(sy < nsy - 1)
    def _():
        for copy in zn_copies:
            copy.wait_recv()


def finish_kernel(
    dims, q, cross, node_own, east_in, north_in, zn, ze, dn, de, ne,
    node_out, east_out, north_out,
    full_v, im_v, pk_v, nrim_v, erim_v, own_sem, int_sem, cross_sem, rim_sem,
):
    fields, xs, ys, m = dims
    half = m // 2
    tiles = [(x, f) for x in range(xs) for f in range(fields)]
    field = lax.axis_index("field")
    own0, oth0 = field * fields, (1 - field) * fields
    copies = []

    def put(src, dst, sem):
        copy = pltpu.make_async_copy(src, dst, sem)
        copy.start()
        copies.append(copy)

    for f in range(fields):
        for g in range(fields):
            put(node_own.at[f, g], node_out.at[f, own0 + g], own_sem.at[f, g])
            put(cross.at[f, g], node_out.at[f, oth0 + g], cross_sem.at[f, g])
    for f in range(fields):
        put(east_in.at[f, : xs - 1], east_out.at[f, : xs - 1], int_sem.at[0, f])
        put(north_in.at[f, :, 0], north_out.at[f, :, 0], int_sem.at[1, f])

    rims = []
    for t, (x, f) in enumerate(tiles):
        rims.append((zn, x, f, q.at[ys - 1, x, f], dn.at[t : t + 1, :]))
    for y in range(ys):
        for f in range(fields):
            rims.append((ze, y, f, q.at[y, xs - 1, f], de.at[y, f : f + 1, :]))
    for r, (z, i, f, _, _) in enumerate(rims):
        turned = z[i].T[f * half : (f + 1) * half, :]
        full_v[r, :half, :half] = z[i, :, f * half : (f + 1) * half]
        full_v[r, half:, :half] = turned
        full_v[r, :half, half:] = turned
        full_v[r, half:, half:] = jnp.zeros((half, half), BF)
    for r in range(len(rims)):
        im_v[r] = (mm(ne[r, :, :m], full_v[r]) + ne[r, :, m:].astype(F32)).astype(BF)
    for r, (_, _, _, tile, _) in enumerate(rims):
        pk_v[r] = (-mm(tile[...], im_v[r])).astype(BF)
    for t, (x, f) in enumerate(tiles):
        nrim_v[f, x] = mm(pk_v[t], coarse_hot(rims[t][4][...], m)).astype(BF)
    for f in range(fields):
        put(nrim_v.at[f], north_out.at[f, :, ys - 1], rim_sem.at[0, f])
    for y in range(ys):
        for f in range(fields):
            r = len(tiles) + y * fields + f
            erim_v[f, y] = mm(pk_v[r], coarse_hot(rims[r][4][...], m)).astype(BF)
    for f in range(fields):
        put(erim_v.at[f], east_out.at[f, xs - 1], rim_sem.at[1, f])
    for copy in copies:
        copy.wait()


def solution(mesh):
    nsx, nsy = mesh.shape["sx"], mesh.shape["sy"]

    def body(inner_block, east_block, north_block, shift_diag, coupling, coarse_flags):
        fields, xs, ys, m = inner_block.shape[:4]
        half = m // 2
        rims = fields * (xs + ys)
        every = coupling.shape[1]
        hbm = pl.BlockSpec(memory_space=pltpu.HBM)
        vmem = pl.BlockSpec(memory_space=pltpu.VMEM)
        dma = pltpu.SemaphoreType.DMA

        def exchange(*refs):
            exchange_kernel((nsx, nsy, fields, xs, ys, m), *refs)

        def finish(*refs):
            finish_kernel((fields, xs, ys, m), *refs)

        mid = pl.pallas_call(
            exchange,
            out_shape=[
                pltpu.VMEM((ys, xs, fields, m, m), BF),
                pltpu.VMEM((fields, fields, xs, ys, m, m), BF),
                pltpu.VMEM((fields, fields, xs, ys, m, m), BF),
                pltpu.VMEM((fields, xs, ys, m, m), BF),
                pltpu.VMEM((fields, xs, ys, m, m), BF),
                pltpu.VMEM((xs, half, m), BF),
                pltpu.VMEM((ys, half, m), BF),
                pltpu.VMEM((PAD, m), F32),
                pltpu.VMEM((ys, 8, m), F32),
                pltpu.VMEM((rims, m, 2 * m), BF),
            ],
            in_specs=[hbm] * 6,
            out_specs=[vmem] * 10,
            scratch_shapes=[
                pltpu.VMEM((ys, fields, xs, m, m), BF),
                pltpu.VMEM((fields, xs, ys, m, m), BF),
                pltpu.VMEM((fields, xs, ys, m, m), BF),
                pltpu.VMEM((fields, xs, ys, m), F32),
                pltpu.VMEM((fields, every, xs, ys, m), F32),
                pltpu.VMEM((fields, xs, ys, m), jnp.int32),
                pltpu.VMEM((ys, xs, fields, m, m), BF),
                pltpu.VMEM((ys, xs, fields, m, m), BF),
                pltpu.VMEM((ys, xs, fields, m, 4 * m), BF),
                pltpu.VMEM((ys, PAD, m), F32),
                pltpu.VMEM((ys, PAD, m), F32),
                pltpu.VMEM((ys, PAD, m), F32),
                pltpu.VMEM((ys, PAD, m), F32),
                pltpu.VMEM((ys, PAD, m), F32),
                pltpu.VMEM((ys, m, m), F32),
                pltpu.VMEM((ys, m, m), F32),
                pltpu.VMEM((ys, PAD, m), F32),
                pltpu.VMEM((ys, PAD, m, m), BF),
                pltpu.VMEM((ys, PAD, m, m), BF),
                pltpu.VMEM((xs, half, m), BF),
                pltpu.VMEM((ys, half, m), BF),
                pltpu.VMEM((m, m), BF),
                pltpu.VMEM((m, m), BF),
                pltpu.VMEM((PAD, m), F32),
                pltpu.VMEM((ys, 8, m), F32),
                pltpu.VMEM((ys, xs, fields, m, m), BF),
                pltpu.VMEM((ys, xs, fields, m, 2 * m), BF),
                pltpu.VMEM((ys, m, m), F32),
                dma((ys,)), dma((3,)), dma((2,)),
                dma((2,)), dma((2,)), dma((ys,)), dma((ys,)), dma((2,)), dma((2,)), dma((ys,)), dma((ys,)),
            ],
            compiler_params=pltpu.CompilerParams(
                collective_id=0, has_side_effects=True, vmem_limit_bytes=32 * MIB
            ),
            name="exchange",
        )(*[
            pltpu.with_memory_space_constraint(a, pltpu.HBM)
            for a in (inner_block, east_block, north_block, shift_diag, coupling, coarse_flags)
        ])

        return pl.pallas_call(
            finish,
            out_shape=[
                jax.ShapeDtypeStruct((fields, every, xs, ys, m, m), BF),
                jax.ShapeDtypeStruct((fields, xs, ys, m, m), BF),
                jax.ShapeDtypeStruct((fields, xs, ys, m, m), BF),
            ],
            in_specs=[vmem] * 10,
            out_specs=[hbm] * 3,
            scratch_shapes=[
                pltpu.VMEM((rims, m, m), BF),
                pltpu.VMEM((rims, m, m), BF),
                pltpu.VMEM((rims, m, m), BF),
                pltpu.VMEM((fields, xs, m, m), BF),
                pltpu.VMEM((fields, ys, m, m), BF),
                dma((fields, fields)), dma((2, fields)), dma((fields, fields)), dma((2, fields)),
            ],
            compiler_params=pltpu.CompilerParams(vmem_limit_bytes=24 * MIB),
            name="finish",
        )(*mid)

    in_specs = (
        P("field", "sx", "sy", None, None),
        P("field", "sx", "sy", None, None),
        P("field", "sx", "sy", None, None),
        P("field", "sx", "sy", None),
        P("field", None, "sx", "sy", None),
        P("field", "sx", "sy", None),
    )
    out_specs = (
        P("field", None, "sx", "sy", None, None),
        P("field", "sx", "sy", None, None),
        P("field", "sx", "sy", None, None),
    )
    return jax.shard_map(body, mesh=mesh, in_specs=in_specs, out_specs=out_specs, check_vma=False)
```

```python
import jax
import jax.numpy as jnp
from jax import lax
from jax.experimental import pallas as pl
from jax.experimental.pallas import tpu as pltpu
from jax.sharding import PartitionSpec as P

BF = jnp.bfloat16
F32 = jnp.float32
MESH = pl.DeviceIdType.MESH
NN = (((1,), (0,)), ((), ()))
NT = (((1,), (1,)), ((), ()))
MIB = 1 << 20
PAD = 24


def mm(left, right, dims=NN):
    return lax.dot_general(left, right, dims, preferred_element_type=F32)


def iota(shape, axis):
    return lax.broadcasted_iota(jnp.int32, shape, axis)


def fine_hot(dest, m):
    return jnp.where(-1.0 - dest == iota((m, m), 0).astype(F32), 1.0, 0.0).astype(BF)


def coarse_hot(dest, m):
    return jnp.where(dest == iota((m, m), 0).astype(F32), 1.0, 0.0).astype(BF)


def exchange_kernel(
    dims, inner, east, north, shift, coupling, flags,
    q_out, other_out, node_out, east_out, north_out, zn_out, ze_out, dn_out, de_out, ne_out, kt_out,
    w_v, e_v, n_v, s_v, k_v, c_v, p_v, w0_v, wt_v, c_r, s_r, a_r, tot_r, str_r, k_r, fac_t, d_v, y_v, x_v,
    zns_v, zes_v, eye_v, off_v, dnr_v, der_v,
    w_sem, vec_sem, en_sem, zs_sem, zr_sem, es_sem, er_sem, ds_sem, dr_sem, ps_sem, pr_sem,
):
    nsx, nsy, fields, xs, ys, m = dims
    half = m // 2
    tiles = [(x, f) for x in range(xs) for f in range(fields)]
    step = -(-xs // 2)
    groups = [(a, min(a + step, xs)) for a in range(0, xs, step)]
    field, sx, sy = lax.axis_index("field"), lax.axis_index("sx"), lax.axis_index("sy")
    barrier = pltpu.get_barrier_semaphore()
    partner = {"field": 1 - field}

    flag_load = pltpu.make_async_copy(flags, c_v, vec_sem.at[0])
    shift_load = pltpu.make_async_copy(shift, s_v, vec_sem.at[1])
    k_load = pltpu.make_async_copy(coupling, k_v, vec_sem.at[2])
    w_loads = [pltpu.make_async_copy(inner.at[:, :, y], w_v.at[y], w_sem.at[y]) for y in range(ys)]
    e_load = pltpu.make_async_copy(east, e_v, en_sem.at[0])
    n_load = pltpu.make_async_copy(north, n_v, en_sem.at[1])
    flag_load.start()
    shift_load.start()
    w_loads[0].start()

    pl.semaphore_signal(barrier, inc=1, device_id=partner, device_id_type=MESH)


    @pl.when(sy < nsy - 1)
    def _():
        pl.semaphore_signal(barrier, inc=1, device_id={"sy": sy + 1}, device_id_type=MESH)

    pl.semaphore_signal(barrier, inc=1, device_id={"sx": lax.rem(sx + 1, nsx)}, device_id_type=MESH)

    unit = iota((m, m), 0) == iota((m, m), 1)
    eye_v[...] = jnp.where(unit, 1.0, 0.0).astype(BF)
    off_v[...] = jnp.where(unit, 0.0, 1.0).astype(BF)

    c_r[...] = jnp.zeros(c_r.shape, F32)
    s_r[...] = jnp.ones(s_r.shape, F32)
    k_r[...] = jnp.zeros(k_r.shape, F32)
    tot_r[...] = jnp.ones(tot_r.shape, F32)
    str_r[...] = jnp.ones(str_r.shape, F32)
    flag_load.wait()
    for t, (x, f) in enumerate(tiles):
        row = c_v[f, x].astype(F32)
        for y in range(ys):
            c_r[y, t : t + 1, :] = row[y : y + 1, :]
    before = jnp.where(iota((m, m), 0) < iota((m, m), 1), 1.0, 0.0).astype(BF)
    for y in range(ys):
        c = c_r[y]
        rank_c = mm(c.astype(BF), before)
        count = jnp.sum(c, axis=1, keepdims=True)
        short = jnp.minimum(count, m - count)
        rank = jnp.where(c > 0.5, rank_c, iota((PAD, m), 1).astype(F32) - rank_c)
        place = jnp.where(rank < half, rank, rank + short)
        d_v[y] = jnp.where(c > 0.5, place, -1.0 - place)


    def to_north(src, dst, send, recv):
        return pltpu.make_async_remote_copy(
            src_ref=src, dst_ref=dst, send_sem=send, recv_sem=recv, device_id={"sy": sy - 1}, device_id_type=MESH)

    def to_east(src, dst, send, recv):
        return pltpu.make_async_remote_copy(
            src_ref=src, dst_ref=dst, send_sem=send, recv_sem=recv, device_id={"sx": lax.rem(sx + nsx - 1, nsx)}, device_id_type=MESH)

    dn_copy = to_north(d_v.at[0], dnr_v, ds_sem.at[0], dr_sem.at[0])
    de_copy = to_east(d_v.at[:, 0:8], der_v, ds_sem.at[1], dr_sem.at[1])
    zn_copies = [to_north(zns_v.at[a:b], zn_out.at[a:b], zs_sem.at[k], zr_sem.at[k]) for k, (a, b) in enumerate(groups)]
    ze_copies = [
        to_east(zns_v.at[0] if y == 0 else zes_v.at[y], ze_out.at[y], es_sem.at[y], er_sem.at[y]) for y in range(ys)
    ]
    p_copies = [
        pltpu.make_async_remote_copy(
            src_ref=p_v.at[y], dst_ref=other_out.at[y], send_sem=ps_sem.at[y], recv_sem=pr_sem.at[y],
            device_id=partner, device_id_type=MESH)
        for y in range(ys)
    ]

    @pl.when(sy == nsy - 1)
    def _():
        dnr_v[...] = jnp.zeros(dnr_v.shape, F32)
        zn_out[...] = jnp.zeros(zn_out.shape, BF)


    def interpolate(y):
        for x in range(xs):
            left = jnp.concatenate(
                [jnp.ones((1, m), F32), c_r[y, x * fields : (x + 1) * fields, :], jnp.zeros((15 - fields, m), F32)], axis=0
            ).astype(BF)
            for f in range(fields):
                t = x * fields + f
                w0 = w_v[y, f, x] * off_v[...]
                w0_v[y, x, f] = w0
                sums = mm(left, w0, NT)
                tot_r[y, t : t + 1, :] = sums[0:1, :]
                str_r[y, t : t + 1, :] = sums[1 + f : 2 + f, :]
        total, c = tot_r[y], c_r[y]
        diag = total + s_r[y]
        alpha = total / jnp.maximum(str_r[y], total * (1.0 / 32.0))
        factor = (1.0 - c) * alpha / diag
        a_r[y] = diag
        fac_t[y] = jnp.concatenate([factor, jnp.zeros((m - PAD, m), F32)], axis=0).T
        for t, (x, f) in enumerate(tiles):
            chosen = jnp.broadcast_to(c_r[y, t : t + 1, :], (m, m)).astype(BF)
            scaled = (fac_t[y, :, t : t + 1] * w0_v[y, x, f].astype(F32)).astype(BF)
            p_v[y, x, f] = scaled * chosen + eye_v[...] * chosen

    def squeeze(y, some):
        for x, f in some:
            t = x * fields + f
            y_v[y, t] = mm(fine_hot(d_v[y, t : t + 1, :], m), p_v[y, x, f]).astype(BF)
        for x, f in some:
            t = x * fields + f
            x_v[y, t] = mm(y_v[y, t], coarse_hot(d_v[y, t : t + 1, :], m), NT).astype(BF)

    def folded(y, x):
        parts = []
        for f in range(fields):
            t = x * fields + f
            turned = x_v[y, t].T
            parts.append(x_v[y, t, :half, :half] + turned[:half, half:] + turned[half:, :half])
        return jnp.concatenate(parts, axis=1)

    prompt = sy != nsy // 2
    shift_load.wait()
    for t, (x, f) in enumerate(tiles):
        row = s_v[f, x]
        for y in range(ys):
            s_r[y, t : t + 1, :] = row[y : y + 1, :]
    w_loads[0].wait()
    for copy in w_loads[1:]:
        copy.start()
    k_load.start()
    e_load.start()
    n_load.start()
    interpolate(0)
    for k, (a, b) in enumerate(groups):
        squeeze(0, tiles[a * fields : b * fields])
        for x in range(a, b):
            zns_v[x] = folded(0, x)

        if k == 0:
            @pl.when(prompt)
            def _():
                pl.semaphore_wait(barrier, jnp.where(sy > 0, 3, 2))

        @pl.when(prompt & (sy > 0))
        def _():
            if k == 0:
                dn_copy.start()
            zn_copies[k].start()

    @pl.when(prompt)
    def _():
        for copy in [de_copy, ze_copies[0], p_copies[0]]:
            copy.start()

    for y in range(1, ys):
        w_loads[y].wait()
        interpolate(y)
        squeeze(y, tiles[:fields])
        zes_v[y] = folded(y, 0)

    @pl.when(prompt)
    def _():
        for copy in ze_copies[1:] + p_copies[1:]:
            copy.start()

    for y in range(ys):
        for x, f in tiles:
            q_out[y, x, f] = p_v[y, x, f].T

    k_load.wait()
    own0, oth0 = field * fields, (1 - field) * fields
    for t, (x, f) in enumerate(tiles):
        rows = [k_v[f, own0 + f, x], k_v[f, own0 + (1 - f), x], k_v[f, oth0, x], k_v[f, oth0 + 1, x]]
        for j, row in enumerate(rows):
            for y in range(ys):
                k_r[y, j * PAD + t : j * PAD + t + 1, :] = row[y : y + 1, :]
    for y in range(ys):
        k_r[y, :PAD, :] = k_r[y, :PAD, :] + a_r[y]
        kt_out[y] = k_r[y].T

    @pl.when(jnp.logical_not(prompt))
    def _():
        pl.semaphore_wait(barrier, 3)
        for copy in [dn_copy, de_copy] + zn_copies + ze_copies + p_copies:
            copy.start()

    e_load.wait()
    n_load.wait()

    def column(j, y, t):
        return kt_out[y, :, j * PAD + t : j * PAD + t + 1]

    for y in range(ys):
        for t, (x, f) in enumerate(tiles):
            p = p_v[y, x, f]
            own = mm(w0_v[y, x, f], p)
            wt_v[y, x, f, :, f * m : (f + 1) * m] = (column(0, y, t) * p.astype(F32) - own).astype(BF)
            wt_v[y, x, f, :, (1 - f) * m : (2 - f) * m] = (column(1, y, t) * p_v[y, x, 1 - f].astype(F32)).astype(BF)
            if x < xs - 1:
                wt_v[y, x, f, :, 2 * m : 3 * m] = mm(e_v[f, x, y], p_v[y, x + 1, f]).astype(BF)
            if y < ys - 1:
                wt_v[y, x, f, :, 3 * m : 4 * m] = mm(n_v[f, x, y], p_v[y + 1, x, f]).astype(BF)
    for y in range(ys):
        for x, f in tiles:
            q = q_out[y, x, f]
            res = mm(q, wt_v[y, x, f, :, : 2 * m])
            for g in range(fields):
                node_out[f, g, x, y] = res[:, g * m : (g + 1) * m].astype(BF)
            if x < xs - 1:
                east_out[f, x, y] = (-mm(q, wt_v[y, x, f, :, 2 * m : 3 * m])).astype(BF)
            if y < ys - 1:
                north_out[f, x, y] = (-mm(q, wt_v[y, x, f, :, 3 * m : 4 * m])).astype(BF)

    @pl.when(sy < nsy - 1)
    def _():
        dn_copy.wait_recv()

    de_copy.wait()
    dn_out[...] = jnp.where(sy < nsy - 1, dnr_v[...], m * 4.0)
    de_out[...] = jnp.where(sx < nsx - 1, der_v[...], m * 4.0)

    def reorder(r, tile, dest):
        ne_out[r] = mm(tile, jnp.concatenate([fine_hot(dest, m), coarse_hot(dest, m)], axis=0), NT).astype(BF)

    for t, (x, f) in enumerate(tiles):
        reorder(t, n_v[f, x, ys - 1], dn_out[t : t + 1, :])
    for y in range(ys):
        for f in range(fields):
            reorder(len(tiles) + y * fields + f, e_v[f, xs - 1, y], de_out[y, f : f + 1, :])

    for copy in p_copies:
        copy.wait()

    for copy in ze_copies:
        copy.wait()

    @pl.when(sy > 0)
    def _():
        for copy in [dn_copy] + zn_copies:
            copy.wait_send()

    @pl.when(sy < nsy - 1)
    def _():
        for copy in zn_copies:
            copy.wait_recv()


def finish_kernel(
    dims, q, other, node_own, east_in, north_in, zn, ze, dn, de, ne, kt,
    node_out, east_out, north_out,
    wt_v, node_v, full_v, im_v, pk_v, nrim_v, erim_v, own_sem, int_sem, cross_sem, rim_sem,
):
    fields, xs, ys, m = dims
    half = m // 2
    tiles = [(x, f) for x in range(xs) for f in range(fields)]
    field = lax.axis_index("field")
    own0, oth0 = field * fields, (1 - field) * fields
    copies = []

    def put(src, dst, sem):
        copy = pltpu.make_async_copy(src, dst, sem)
        copy.start()
        copies.append(copy)

    for f in range(fields):
        for g in range(fields):
            put(node_own.at[f, g], node_out.at[f, own0 + g], own_sem.at[f, g])
    for f in range(fields):
        put(east_in.at[f, : xs - 1], east_out.at[f, : xs - 1], int_sem.at[0, f])
        put(north_in.at[f, :, 0], north_out.at[f, :, 0], int_sem.at[1, f])

    def column(j, y, t):
        return kt[y, :, j * PAD + t : j * PAD + t + 1]

    for y in range(ys):
        for t, (x, f) in enumerate(tiles):
            for g in range(fields):
                wt_v[y, x, f, :, g * m : (g + 1) * m] = (column(2 + g, y, t) * other[y, x, g].astype(F32)).astype(BF)
    for x in range(xs):
        for f in range(fields):
            for y in range(ys):
                res = mm(q[y, x, f], wt_v[y, x, f])
                for g in range(fields):
                    node_v[f, g, x, y] = res[:, g * m : (g + 1) * m].astype(BF)
            for g in range(fields):
                put(node_v.at[f, g, x], node_out.at[f, oth0 + g, x], cross_sem.at[f, g, x])

    rims = []
    for t, (x, f) in enumerate(tiles):
        rims.append((zn, x, f, q.at[ys - 1, x, f], dn.at[t : t + 1, :]))
    for y in range(ys):
        for f in range(fields):
            rims.append((ze, y, f, q.at[y, xs - 1, f], de.at[y, f : f + 1, :]))
    for r, (z, i, f, _, _) in enumerate(rims):
        turned = z[i].T[f * half : (f + 1) * half, :]
        full_v[r, :half, :half] = z[i, :, f * half : (f + 1) * half]
        full_v[r, half:, :half] = turned
        full_v[r, :half, half:] = turned
        full_v[r, half:, half:] = jnp.zeros((half, half), BF)
    for r in range(len(rims)):
        im_v[r] = (mm(ne[r, :, :m], full_v[r]) + ne[r, :, m:].astype(F32)).astype(BF)
    for r, (_, _, _, tile, _) in enumerate(rims):
        pk_v[r] = (-mm(tile[...], im_v[r])).astype(BF)
    for y in range(ys):
        for f in range(fields):
            r = len(tiles) + y * fields + f
            erim_v[f, y] = mm(pk_v[r], coarse_hot(rims[r][4][...], m)).astype(BF)
    for f in range(fields):
        put(erim_v.at[f], east_out.at[f, xs - 1], rim_sem.at[1, f])
    for f in range(fields):
        for x in range(xs):
            t = x * fields + f
            nrim_v[f, x] = mm(pk_v[t], coarse_hot(rims[t][4][...], m)).astype(BF)
        put(nrim_v.at[f], north_out.at[f, :, ys - 1], rim_sem.at[0, f])
    for copy in copies:
        copy.wait()


def solution(mesh):
    nsx, nsy = mesh.shape["sx"], mesh.shape["sy"]

    def body(inner_block, east_block, north_block, shift_diag, coupling, coarse_flags):
        fields, xs, ys, m = inner_block.shape[:4]
        half = m // 2
        rims = fields * (xs + ys)
        every = coupling.shape[1]
        hbm = pl.BlockSpec(memory_space=pltpu.HBM)
        vmem = pl.BlockSpec(memory_space=pltpu.VMEM)
        dma = pltpu.SemaphoreType.DMA

        def exchange(*refs):
            exchange_kernel((nsx, nsy, fields, xs, ys, m), *refs)

        def finish(*refs):
            finish_kernel((fields, xs, ys, m), *refs)

        mid = pl.pallas_call(
            exchange,
            out_shape=[
                pltpu.VMEM((ys, xs, fields, m, m), BF),
                pltpu.VMEM((ys, xs, fields, m, m), BF),
                pltpu.VMEM((fields, fields, xs, ys, m, m), BF),
                pltpu.VMEM((fields, xs, ys, m, m), BF),
                pltpu.VMEM((fields, xs, ys, m, m), BF),
                pltpu.VMEM((xs, half, m), BF),
                pltpu.VMEM((ys, half, m), BF),
                pltpu.VMEM((PAD, m), F32),
                pltpu.VMEM((ys, 8, m), F32),
                pltpu.VMEM((rims, m, 2 * m), BF),
                pltpu.VMEM((ys, m, m), F32),
            ],
            in_specs=[hbm] * 6,
            out_specs=[vmem] * 11,
            scratch_shapes=[
                pltpu.VMEM((ys, fields, xs, m, m), BF),
                pltpu.VMEM((fields, xs, ys, m, m), BF),
                pltpu.VMEM((fields, xs, ys, m, m), BF),
                pltpu.VMEM((fields, xs, ys, m), F32),
                pltpu.VMEM((fields, every, xs, ys, m), F32),
                pltpu.VMEM((fields, xs, ys, m), jnp.int32),
                pltpu.VMEM((ys, xs, fields, m, m), BF),
                pltpu.VMEM((ys, xs, fields, m, m), BF),
                pltpu.VMEM((ys, xs, fields, m, 4 * m), BF),
                pltpu.VMEM((ys, PAD, m), F32),
                pltpu.VMEM((ys, PAD, m), F32),
                pltpu.VMEM((ys, PAD, m), F32),
                pltpu.VMEM((ys, PAD, m), F32),
                pltpu.VMEM((ys, PAD, m), F32),
                pltpu.VMEM((ys, m, m), F32),
                pltpu.VMEM((ys, m, m), F32),
                pltpu.VMEM((ys, PAD, m), F32),
                pltpu.VMEM((ys, PAD, m, m), BF),
                pltpu.VMEM((ys, PAD, m, m), BF),
                pltpu.VMEM((xs, half, m), BF),
                pltpu.VMEM((ys, half, m), BF),
                pltpu.VMEM((m, m), BF),
                pltpu.VMEM((m, m), BF),
                pltpu.VMEM((PAD, m), F32),
                pltpu.VMEM((ys, 8, m), F32),
                dma((ys,)), dma((3,)), dma((2,)),
                dma((2,)), dma((2,)), dma((ys,)), dma((ys,)), dma((2,)), dma((2,)), dma((ys,)), dma((ys,)),
            ],
            compiler_params=pltpu.CompilerParams(
                collective_id=0, has_side_effects=True, vmem_limit_bytes=32 * MIB
            ),
            name="exchange",
        )(*[
            pltpu.with_memory_space_constraint(a, pltpu.HBM)
            for a in (inner_block, east_block, north_block, shift_diag, coupling, coarse_flags)
        ])

        return pl.pallas_call(
            finish,
            out_shape=[
                jax.ShapeDtypeStruct((fields, every, xs, ys, m, m), BF),
                jax.ShapeDtypeStruct((fields, xs, ys, m, m), BF),
                jax.ShapeDtypeStruct((fields, xs, ys, m, m), BF),
            ],
            in_specs=[vmem] * 11,
            out_specs=[hbm] * 3,
            scratch_shapes=[
                pltpu.VMEM((ys, xs, fields, m, 2 * m), BF),
                pltpu.VMEM((fields, fields, xs, ys, m, m), BF),
                pltpu.VMEM((rims, m, m), BF),
                pltpu.VMEM((rims, m, m), BF),
                pltpu.VMEM((rims, m, m), BF),
                pltpu.VMEM((fields, xs, m, m), BF),
                pltpu.VMEM((fields, ys, m, m), BF),
                dma((fields, fields)), dma((2, fields)), dma((fields, fields, xs)), dma((2, fields)),
            ],
            compiler_params=pltpu.CompilerParams(vmem_limit_bytes=24 * MIB),
            name="finish",
        )(*mid)

    in_specs = (
        P("field", "sx", "sy", None, None),
        P("field", "sx", "sy", None, None),
        P("field", "sx", "sy", None, None),
        P("field", "sx", "sy", None),
        P("field", None, "sx", "sy", None),
        P("field", "sx", "sy", None),
    )
    out_specs = (
        P("field", None, "sx", "sy", None, None),
        P("field", "sx", "sy", None, None),
        P("field", "sx", "sy", None, None),
    )
    return jax.shard_map(body, mesh=mesh, in_specs=in_specs, out_specs=out_specs, check_vma=False)
```

```python
import jax
import jax.numpy as jnp
from jax import lax
from jax.experimental import pallas as pl
from jax.experimental.pallas import tpu as pltpu
from jax.sharding import PartitionSpec as P

BF = jnp.bfloat16
F32 = jnp.float32
MESH = pl.DeviceIdType.MESH
NN = (((1,), (0,)), ((), ()))
NT = (((1,), (1,)), ((), ()))
MIB = 1 << 20
PAD = 24


def mm(left, right, dims=NN):
    return lax.dot_general(left, right, dims, preferred_element_type=F32)


def iota(shape, axis):
    return lax.broadcasted_iota(jnp.int32, shape, axis)


def fine_hot(dest, m):
    return jnp.where(-1.0 - dest == iota((m, m), 0).astype(F32), 1.0, 0.0).astype(BF)


def coarse_hot(dest, m):
    return jnp.where(dest == iota((m, m), 0).astype(F32), 1.0, 0.0).astype(BF)


def exchange_kernel(
    dims, inner, east, north, shift, coupling, flags,
    q_out, other_out, node_out, east_out, north_out, zn_out, ze_out, dn_out, de_out, ne_out, kt_out,
    w_v, e_v, n_v, s_v, k_v, c_v, p_v, w0_v, wt_v, c_r, s_r, a_r, tot_r, str_r, k_r, fac_t, d_v, y_v, x_v,
    zns_v, zes_v, eye_v, off_v, dnr_v, der_v,
    w_sem, vec_sem, en_sem, zs_sem, zr_sem, es_sem, er_sem, ds_sem, dr_sem, ps_sem, pr_sem,
):
    nsx, nsy, fields, xs, ys, m = dims
    half = m // 2
    tiles = [(x, f) for x in range(xs) for f in range(fields)]
    step = -(-xs // 2)
    groups = [(a, min(a + step, xs)) for a in range(0, xs, step)]
    field, sx, sy = lax.axis_index("field"), lax.axis_index("sx"), lax.axis_index("sy")
    barrier = pltpu.get_barrier_semaphore()
    partner = {"field": 1 - field}

    flag_load = pltpu.make_async_copy(flags, c_v, vec_sem.at[0])
    shift_load = pltpu.make_async_copy(shift, s_v, vec_sem.at[1])
    k_load = pltpu.make_async_copy(coupling, k_v, vec_sem.at[2])
    w_loads = [pltpu.make_async_copy(inner.at[:, :, y], w_v.at[y], w_sem.at[y]) for y in range(ys)]
    e_load = pltpu.make_async_copy(east, e_v, en_sem.at[0])
    n_load = pltpu.make_async_copy(north, n_v, en_sem.at[1])
    flag_load.start()
    shift_load.start()
    w_loads[0].start()

    pl.semaphore_signal(barrier, inc=1, device_id=partner, device_id_type=MESH)


    @pl.when(sy < nsy - 1)
    def _():
        pl.semaphore_signal(barrier, inc=1, device_id={"sy": sy + 1}, device_id_type=MESH)

    pl.semaphore_signal(barrier, inc=1, device_id={"sx": lax.rem(sx + 1, nsx)}, device_id_type=MESH)

    unit = iota((m, m), 0) == iota((m, m), 1)
    eye_v[...] = jnp.where(unit, 1.0, 0.0).astype(BF)
    off_v[...] = jnp.where(unit, 0.0, 1.0).astype(BF)

    c_r[...] = jnp.zeros(c_r.shape, F32)
    s_r[...] = jnp.ones(s_r.shape, F32)
    k_r[...] = jnp.zeros(k_r.shape, F32)
    tot_r[...] = jnp.ones(tot_r.shape, F32)
    str_r[...] = jnp.ones(str_r.shape, F32)
    flag_load.wait()
    for t, (x, f) in enumerate(tiles):
        row = c_v[f, x].astype(F32)
        for y in range(ys):
            c_r[y, t : t + 1, :] = row[y : y + 1, :]
    before = jnp.where(iota((m, m), 0) < iota((m, m), 1), 1.0, 0.0).astype(BF)
    for y in range(ys):
        c = c_r[y]
        rank_c = mm(c.astype(BF), before)
        count = jnp.sum(c, axis=1, keepdims=True)
        short = jnp.minimum(count, m - count)
        rank = jnp.where(c > 0.5, rank_c, iota((PAD, m), 1).astype(F32) - rank_c)
        place = jnp.where(rank < half, rank, rank + short)
        d_v[y] = jnp.where(c > 0.5, place, -1.0 - place)


    def to_north(src, dst, send, recv):
        return pltpu.make_async_remote_copy(
            src_ref=src, dst_ref=dst, send_sem=send, recv_sem=recv, device_id={"sy": sy - 1}, device_id_type=MESH)

    def to_east(src, dst, send, recv):
        return pltpu.make_async_remote_copy(
            src_ref=src, dst_ref=dst, send_sem=send, recv_sem=recv, device_id={"sx": lax.rem(sx + nsx - 1, nsx)}, device_id_type=MESH)

    dn_copy = to_north(d_v.at[0], dnr_v, ds_sem.at[0], dr_sem.at[0])
    de_copy = to_east(d_v.at[:, 0:8], der_v, ds_sem.at[1], dr_sem.at[1])
    zn_copies = [to_north(zns_v.at[a:b], zn_out.at[a:b], zs_sem.at[k], zr_sem.at[k]) for k, (a, b) in enumerate(groups)]
    ze_copies = [
        to_east(zns_v.at[0] if y == 0 else zes_v.at[y], ze_out.at[y], es_sem.at[y], er_sem.at[y]) for y in range(ys)
    ]
    p_copies = [
        pltpu.make_async_remote_copy(
            src_ref=p_v.at[y], dst_ref=other_out.at[y], send_sem=ps_sem.at[y], recv_sem=pr_sem.at[y],
            device_id=partner, device_id_type=MESH)
        for y in range(ys)
    ]

    @pl.when(sy == nsy - 1)
    def _():
        dnr_v[...] = jnp.zeros(dnr_v.shape, F32)
        zn_out[...] = jnp.zeros(zn_out.shape, BF)


    def interpolate(y):
        for x in range(xs):
            left = jnp.concatenate(
                [jnp.ones((1, m), F32), c_r[y, x * fields : (x + 1) * fields, :], jnp.zeros((15 - fields, m), F32)], axis=0
            ).astype(BF)
            for f in range(fields):
                t = x * fields + f
                w0 = w_v[y, f, x] * off_v[...]
                w0_v[y, x, f] = w0
                sums = mm(left, w0, NT)
                tot_r[y, t : t + 1, :] = sums[0:1, :]
                str_r[y, t : t + 1, :] = sums[1 + f : 2 + f, :]
        total, c = tot_r[y], c_r[y]
        diag = total + s_r[y]
        alpha = total / jnp.maximum(str_r[y], total * (1.0 / 32.0))
        factor = (1.0 - c) * alpha / diag
        a_r[y] = diag
        fac_t[y] = jnp.concatenate([factor, jnp.zeros((m - PAD, m), F32)], axis=0).T
        for t, (x, f) in enumerate(tiles):
            chosen = jnp.broadcast_to(c_r[y, t : t + 1, :], (m, m)).astype(BF)
            scaled = (fac_t[y, :, t : t + 1] * w0_v[y, x, f].astype(F32)).astype(BF)
            p_v[y, x, f] = scaled * chosen + eye_v[...] * chosen

    def squeeze(y, some):
        for x, f in some:
            t = x * fields + f
            y_v[y, t] = mm(fine_hot(d_v[y, t : t + 1, :], m), p_v[y, x, f]).astype(BF)
        for x, f in some:
            t = x * fields + f
            x_v[y, t] = mm(y_v[y, t], coarse_hot(d_v[y, t : t + 1, :], m), NT).astype(BF)

    def folded(y, x):
        parts = []
        for f in range(fields):
            t = x * fields + f
            turned = x_v[y, t].T
            parts.append(x_v[y, t, :half, :half] + turned[:half, half:] + turned[half:, :half])
        return jnp.concatenate(parts, axis=1)

    prompt = sy != nsy // 2
    shift_load.wait()
    for t, (x, f) in enumerate(tiles):
        row = s_v[f, x]
        for y in range(ys):
            s_r[y, t : t + 1, :] = row[y : y + 1, :]
    w_loads[0].wait()
    for copy in w_loads[1:]:
        copy.start()
    k_load.start()
    e_load.start()
    n_load.start()
    interpolate(0)
    for k, (a, b) in enumerate(groups):
        squeeze(0, tiles[a * fields : b * fields])
        for x in range(a, b):
            zns_v[x] = folded(0, x)

        if k == 0:
            @pl.when(prompt)
            def _():
                pl.semaphore_wait(barrier, jnp.where(sy > 0, 3, 2))

        @pl.when(prompt & (sy > 0))
        def _():
            if k == 0:
                dn_copy.start()
            zn_copies[k].start()

    @pl.when(prompt)
    def _():
        for copy in [de_copy, ze_copies[0], p_copies[0]]:
            copy.start()

    for y in range(1, ys):
        w_loads[y].wait()
        interpolate(y)
        squeeze(y, tiles[:fields])
        zes_v[y] = folded(y, 0)

    @pl.when(prompt)
    def _():
        for copy in ze_copies[1:] + p_copies[1:]:
            copy.start()

    for y in range(ys):
        for x, f in tiles:
            q_out[y, x, f] = p_v[y, x, f].T

    k_load.wait()
    own0, oth0 = field * fields, (1 - field) * fields
    for t, (x, f) in enumerate(tiles):
        rows = [k_v[f, own0 + f, x], k_v[f, own0 + (1 - f), x], k_v[f, oth0, x], k_v[f, oth0 + 1, x]]
        for j, row in enumerate(rows):
            for y in range(ys):
                k_r[y, j * PAD + t : j * PAD + t + 1, :] = row[y : y + 1, :]
    for y in range(ys):
        k_r[y, :PAD, :] = k_r[y, :PAD, :] + a_r[y]
        kt_out[y] = k_r[y].T

    @pl.when(jnp.logical_not(prompt))
    def _():
        pl.semaphore_wait(barrier, 3)
        for copy in [dn_copy, de_copy] + zn_copies + ze_copies + p_copies:
            copy.start()

    e_load.wait()
    n_load.wait()

    def column(j, y, t):
        return kt_out[y, :, j * PAD + t : j * PAD + t + 1]

    for y in range(ys):
        for t, (x, f) in enumerate(tiles):
            p = p_v[y, x, f]
            own = mm(w0_v[y, x, f], p)
            wt_v[y, x, f, :, f * m : (f + 1) * m] = (column(0, y, t) * p.astype(F32) - own).astype(BF)
            wt_v[y, x, f, :, (1 - f) * m : (2 - f) * m] = (column(1, y, t) * p_v[y, x, 1 - f].astype(F32)).astype(BF)
            if x < xs - 1:
                wt_v[y, x, f, :, 2 * m : 3 * m] = mm(e_v[f, x, y], p_v[y, x + 1, f]).astype(BF)
            if y < ys - 1:
                wt_v[y, x, f, :, 3 * m : 4 * m] = mm(n_v[f, x, y], p_v[y + 1, x, f]).astype(BF)
    for y in range(ys):
        for x, f in tiles:
            q = q_out[y, x, f]
            res = mm(q, wt_v[y, x, f, :, : 2 * m])
            for g in range(fields):
                node_out[f, g, x, y] = res[:, g * m : (g + 1) * m].astype(BF)
            if x < xs - 1:
                east_out[f, x, y] = (-mm(q, wt_v[y, x, f, :, 2 * m : 3 * m])).astype(BF)
            if y < ys - 1:
                north_out[f, x, y] = (-mm(q, wt_v[y, x, f, :, 3 * m : 4 * m])).astype(BF)

    @pl.when(sy < nsy - 1)
    def _():
        dn_copy.wait_recv()

    de_copy.wait()
    dn_out[...] = jnp.where(sy < nsy - 1, dnr_v[...], m * 4.0)
    de_out[...] = jnp.where(sx < nsx - 1, der_v[...], m * 4.0)

    def reorder(r, tile, dest):
        ne_out[r] = mm(tile, jnp.concatenate([fine_hot(dest, m), coarse_hot(dest, m)], axis=0), NT).astype(BF)

    for t, (x, f) in enumerate(tiles):
        reorder(t, n_v[f, x, ys - 1], dn_out[t : t + 1, :])
    for y in range(ys):
        for f in range(fields):
            reorder(len(tiles) + y * fields + f, e_v[f, xs - 1, y], de_out[y, f : f + 1, :])

    for copy in p_copies:
        copy.wait()

    for copy in ze_copies:
        copy.wait()

    @pl.when(sy > 0)
    def _():
        for copy in [dn_copy] + zn_copies:
            copy.wait_send()

    @pl.when(sy < nsy - 1)
    def _():
        for copy in zn_copies:
            copy.wait_recv()


def finish_kernel(
    dims, q, other, node_own, east_in, north_in, zn, ze, dn, de, ne, kt,
    node_out, east_out, north_out,
    wt_v, node_v, full_v, im_v, pk_v, nrim_v, erim_v, own_sem, int_sem, cross_sem, rim_sem,
):
    fields, xs, ys, m = dims
    half = m // 2
    tiles = [(x, f) for x in range(xs) for f in range(fields)]
    field = lax.axis_index("field")
    own0, oth0 = field * fields, (1 - field) * fields
    copies = []

    def put(src, dst, sem):
        copy = pltpu.make_async_copy(src, dst, sem)
        copy.start()
        copies.append(copy)

    for f in range(fields):
        for g in range(fields):
            put(node_own.at[f, g], node_out.at[f, own0 + g], own_sem.at[f, g])
    for f in range(fields):
        put(east_in.at[f, : xs - 1], east_out.at[f, : xs - 1], int_sem.at[0, f])
        put(north_in.at[f, :, 0], north_out.at[f, :, 0], int_sem.at[1, f])

    def column(j, y, t):
        return kt[y, :, j * PAD + t : j * PAD + t + 1]

    for y in range(ys):
        for t, (x, f) in enumerate(tiles):
            for g in range(fields):
                wt_v[y, x, f, :, g * m : (g + 1) * m] = (column(2 + g, y, t) * other[y, x, g].astype(F32)).astype(BF)
    rims = []
    for t, (x, f) in enumerate(tiles):
        rims.append((zn, x, f, q.at[ys - 1, x, f], dn.at[t : t + 1, :]))
    for y in range(ys):
        for f in range(fields):
            rims.append((ze, y, f, q.at[y, xs - 1, f], de.at[y, f : f + 1, :]))
    for r, (z, i, f, _, _) in enumerate(rims):
        turned = z[i].T[f * half : (f + 1) * half, :]
        full_v[r, :half, :half] = z[i, :, f * half : (f + 1) * half]
        full_v[r, half:, :half] = turned
        full_v[r, :half, half:] = turned
        full_v[r, half:, half:] = jnp.zeros((half, half), BF)
    for r in range(len(rims)):
        im_v[r] = (mm(ne[r, :, :m], full_v[r]) + ne[r, :, m:].astype(F32)).astype(BF)
    for x in range(xs):
        for f in range(fields):
            for y in range(ys):
                res = mm(q[y, x, f], wt_v[y, x, f])
                for g in range(fields):
                    node_v[f, g, x, y] = res[:, g * m : (g + 1) * m].astype(BF)
            for g in range(fields):
                put(node_v.at[f, g, x], node_out.at[f, oth0 + g, x], cross_sem.at[f, g, x])

    for r, (_, _, _, tile, _) in enumerate(rims):
        pk_v[r] = (-mm(tile[...], im_v[r])).astype(BF)
    for y in range(ys):
        for f in range(fields):
            r = len(tiles) + y * fields + f
            erim_v[f, y] = mm(pk_v[r], coarse_hot(rims[r][4][...], m)).astype(BF)
    for f in range(fields):
        put(erim_v.at[f], east_out.at[f, xs - 1], rim_sem.at[1, f])
    for f in range(fields):
        for x in range(xs):
            t = x * fields + f
            nrim_v[f, x] = mm(pk_v[t], coarse_hot(rims[t][4][...], m)).astype(BF)
        put(nrim_v.at[f], north_out.at[f, :, ys - 1], rim_sem.at[0, f])
    for copy in copies:
        copy.wait()


def solution(mesh):
    nsx, nsy = mesh.shape["sx"], mesh.shape["sy"]

    def body(inner_block, east_block, north_block, shift_diag, coupling, coarse_flags):
        fields, xs, ys, m = inner_block.shape[:4]
        half = m // 2
        rims = fields * (xs + ys)
        every = coupling.shape[1]
        hbm = pl.BlockSpec(memory_space=pltpu.HBM)
        vmem = pl.BlockSpec(memory_space=pltpu.VMEM)
        dma = pltpu.SemaphoreType.DMA

        def exchange(*refs):
            exchange_kernel((nsx, nsy, fields, xs, ys, m), *refs)

        def finish(*refs):
            finish_kernel((fields, xs, ys, m), *refs)

        mid = pl.pallas_call(
            exchange,
            out_shape=[
                pltpu.VMEM((ys, xs, fields, m, m), BF),
                pltpu.VMEM((ys, xs, fields, m, m), BF),
                pltpu.VMEM((fields, fields, xs, ys, m, m), BF),
                pltpu.VMEM((fields, xs, ys, m, m), BF),
                pltpu.VMEM((fields, xs, ys, m, m), BF),
                pltpu.VMEM((xs, half, m), BF),
                pltpu.VMEM((ys, half, m), BF),
                pltpu.VMEM((PAD, m), F32),
                pltpu.VMEM((ys, 8, m), F32),
                pltpu.VMEM((rims, m, 2 * m), BF),
                pltpu.VMEM((ys, m, m), F32),
            ],
            in_specs=[hbm] * 6,
            out_specs=[vmem] * 11,
            scratch_shapes=[
                pltpu.VMEM((ys, fields, xs, m, m), BF),
                pltpu.VMEM((fields, xs, ys, m, m), BF),
                pltpu.VMEM((fields, xs, ys, m, m), BF),
                pltpu.VMEM((fields, xs, ys, m), F32),
                pltpu.VMEM((fields, every, xs, ys, m), F32),
                pltpu.VMEM((fields, xs, ys, m), jnp.int32),
                pltpu.VMEM((ys, xs, fields, m, m), BF),
                pltpu.VMEM((ys, xs, fields, m, m), BF),
                pltpu.VMEM((ys, xs, fields, m, 4 * m), BF),
                pltpu.VMEM((ys, PAD, m), F32),
                pltpu.VMEM((ys, PAD, m), F32),
                pltpu.VMEM((ys, PAD, m), F32),
                pltpu.VMEM((ys, PAD, m), F32),
                pltpu.VMEM((ys, PAD, m), F32),
                pltpu.VMEM((ys, m, m), F32),
                pltpu.VMEM((ys, m, m), F32),
                pltpu.VMEM((ys, PAD, m), F32),
                pltpu.VMEM((ys, PAD, m, m), BF),
                pltpu.VMEM((ys, PAD, m, m), BF),
                pltpu.VMEM((xs, half, m), BF),
                pltpu.VMEM((ys, half, m), BF),
                pltpu.VMEM((m, m), BF),
                pltpu.VMEM((m, m), BF),
                pltpu.VMEM((PAD, m), F32),
                pltpu.VMEM((ys, 8, m), F32),
                dma((ys,)), dma((3,)), dma((2,)),
                dma((2,)), dma((2,)), dma((ys,)), dma((ys,)), dma((2,)), dma((2,)), dma((ys,)), dma((ys,)),
            ],
            compiler_params=pltpu.CompilerParams(
                collective_id=0, has_side_effects=True, vmem_limit_bytes=32 * MIB
            ),
            name="exchange",
        )(*[
            pltpu.with_memory_space_constraint(a, pltpu.HBM)
            for a in (inner_block, east_block, north_block, shift_diag, coupling, coarse_flags)
        ])

        return pl.pallas_call(
            finish,
            out_shape=[
                jax.ShapeDtypeStruct((fields, every, xs, ys, m, m), BF),
                jax.ShapeDtypeStruct((fields, xs, ys, m, m), BF),
                jax.ShapeDtypeStruct((fields, xs, ys, m, m), BF),
            ],
            in_specs=[vmem] * 11,
            out_specs=[hbm] * 3,
            scratch_shapes=[
                pltpu.VMEM((ys, xs, fields, m, 2 * m), BF),
                pltpu.VMEM((fields, fields, xs, ys, m, m), BF),
                pltpu.VMEM((rims, m, m), BF),
                pltpu.VMEM((rims, m, m), BF),
                pltpu.VMEM((rims, m, m), BF),
                pltpu.VMEM((fields, xs, m, m), BF),
                pltpu.VMEM((fields, ys, m, m), BF),
                dma((fields, fields)), dma((2, fields)), dma((fields, fields, xs)), dma((2, fields)),
            ],
            compiler_params=pltpu.CompilerParams(vmem_limit_bytes=24 * MIB),
            name="finish",
        )(*mid)

    in_specs = (
        P("field", "sx", "sy", None, None),
        P("field", "sx", "sy", None, None),
        P("field", "sx", "sy", None, None),
        P("field", "sx", "sy", None),
        P("field", None, "sx", "sy", None),
        P("field", "sx", "sy", None),
    )
    out_specs = (
        P("field", None, "sx", "sy", None, None),
        P("field", "sx", "sy", None, None),
        P("field", "sx", "sy", None, None),
    )
    return jax.shard_map(body, mesh=mesh, in_specs=in_specs, out_specs=out_specs, check_vma=False)
```
